768 devices in a mesh: blk: 48 (over y, z_hi, core), grp: 16 (over x, z_lo).
Axes of the slice: x: 4, y: 8, z: 12 (z_hi: 3, z_lo: 4; z = z_hi * 4 + z_lo), core: 2. Of those that a mesh axis runs over, the one named last changes fastest.
Arguments:
- images: bfloat16 [110592, 1152], P(('blk', 'grp')), may hold values from -0.17675781 to 0.17675781
- texts: bfloat16 [110592, 1152], P(('blk', 'grp')), may hold values from -0.17675781 to 0.17675781
Outputs:
- row_loss: float32 [110592], P(('blk', 'grp'))
- image_grad: float32 [110592, 1152], P(('blk', 'grp'))
- text_grad: float32 [110592, 1152], P(('blk', 'grp'))
The draws below stay inside these ranges and needn't reach their ends.
All inputs are finite; a program needn't handle non-finite values.
Results may differ from the reference program's by a relative error of at most 0.022.
Values may be sent and summed in bfloat16 or wider, within the bound.
No kernel may reach another device: no remote copies, remote signals or barrier semaphores. Data moves between devices by JAX's collectives and lax.ppermute only.
A program may use at most 64 MiB of HBM per device.

```python
import jax
import jax.numpy as jnp
from jax import lax

D = 1152
ROWS = 144
STEPS = 2
BATCH = 110592
N_BLK = 48
N_GRP = 16


def block_scale(stream_key, dims, cuts, least, top_value):
    factor_of, own = 1.0, jax.random.fold_in(stream_key, 6)
    for axis_at, parts in cuts:
        heights = jnp.exp(jax.random.uniform(jax.random.fold_in(own, axis_at), (parts,), jnp.float32, least / len(cuts), top_value / len(cuts)))
        factor_of = factor_of * jnp.repeat(heights, dims[axis_at] // parts).reshape([-1 if axis == axis_at else 1 for axis in range(len(dims))])
    return factor_of


def scatter_about(own_key, extent, deviation, bound, cuts=(), kind=jnp.bfloat16):
    loudness = block_scale(own_key, extent, cuts, -0.22, 0.18) if cuts else 1.0
    result = jax.random.normal(own_key, extent, jnp.float32) * deviation * loudness
    return jnp.minimum(jnp.maximum(result, -bound), bound).astype(kind)


def setup_inputs(seed: int = 0) -> dict:
    key_list = jax.random.split(jax.random.key(seed), 3)
    images = scatter_about(key_list[0], (BATCH, D), (D ** -0.5), 0.17675781, ((0, 768),))
    texts = scatter_about(key_list[1], (BATCH, D), (D ** -0.5), 0.17675781, ((0, 768),))
    return dict(images=images, texts=texts)


multiplicative_scaling_factor = 10.0
additive_shift_term = -2.0
epsilon = 1e-06

def normalize(values_in):
    widened = values_in.astype(jnp.float32)
    length = jnp.sqrt(lax.optimization_barrier(jnp.sum(widened * widened, axis=-1, keepdims=True)) + epsilon)
    return (widened / length, length)

def project(unit_rows, length, grads):
    radial = lax.optimization_barrier(jnp.sum(unit_rows * grads, axis=-1, keepdims=True))
    return (grads - unit_rows * radial) / length

def reference(images, texts):
    img_unit, img_len = normalize(images)
    txt_unit, txt_len = normalize(texts)
    image_lower_bound = img_unit.astype(jnp.bfloat16)
    txt_low = txt_unit.astype(jnp.bfloat16)
    features = images.shape[1]
    blocks = N_BLK
    block_rows = ROWS * N_GRP
    img_blocks = image_lower_bound.reshape(blocks, block_rows, features)
    txt_blocks = txt_low.reshape(blocks, block_rows, features)
    row_ids = lax.broadcasted_iota(jnp.int32, (block_rows, block_rows), 0)
    column_ids = lax.broadcasted_iota(jnp.int32, (block_rows, block_rows), 1)
    matches = row_ids == column_ids

    def one_block(totals, position):
        picture_entry_slab = lax.dynamic_index_in_dim(img_blocks, position, 0, keepdims=False)
        img_grad = jnp.zeros((block_rows, features), jnp.float32)
        losses = jnp.zeros((block_rows,), jnp.float32)
        for offset in range(STEPS):
            source = ((position - offset) % blocks).astype(jnp.int32)
            leftover_entries = lax.dynamic_index_in_dim(txt_blocks, source, 0, keepdims=False)
            similarity_matrix = jnp.dot(picture_entry_slab, leftover_entries.T, preferred_element_type=jnp.float32) * multiplicative_scaling_factor + additive_shift_term
            if offset == 0:
                match_target_signs = jnp.where(matches, 1.0, -1.0).astype(jnp.float32)
            else:
                match_target_signs = -jnp.ones_like(similarity_matrix)
            losses = losses + lax.optimization_barrier(jnp.sum(jax.nn.softplus(-match_target_signs * similarity_matrix), axis=1))
            logistic_derivatives = (-match_target_signs * jax.nn.sigmoid(-match_target_signs * similarity_matrix) * multiplicative_scaling_factor).astype(jnp.bfloat16)
            img_grad = img_grad + jnp.dot(logistic_derivatives, leftover_entries, preferred_element_type=jnp.float32)
            pieces = jnp.einsum('grm,grd->gmd', logistic_derivatives.reshape(N_GRP, ROWS, block_rows).astype(jnp.float32), picture_entry_slab.reshape(N_GRP, ROWS, features).astype(jnp.float32))
            rounded = lax.optimization_barrier(pieces.astype(jnp.bfloat16))
            summed = lax.optimization_barrier(jnp.sum(rounded.astype(jnp.float32), axis=0))
            totals = totals.at[source].add(summed)
        return (totals, (img_grad, losses))
    start = jnp.zeros((blocks, block_rows, features), jnp.float32)
    totals, (img_grads, losses) = lax.scan(one_block, start, jnp.arange(blocks, dtype=jnp.int32))
    image_grad = project(img_unit, img_len, img_grads.reshape(-1, features))
    text_grad = project(txt_unit, txt_len, totals.reshape(-1, features))
    return (losses.reshape(-1), image_grad, text_grad)
```

```python
import functools

import jax
import jax.numpy as jnp
from jax import lax
from jax.experimental import pallas as pl
from jax.experimental.pallas import tpu as pltpu
from jax.sharding import Mesh
from jax.sharding import PartitionSpec as P

SCALE = 10.0
SHIFT = -2.0
EPS = 1e-06
CORES, NX, NZ = 2, 4, 4
BLK, GRP = ("g", "core"), ("x", "z")
F32, BF16 = jnp.float32, jnp.bfloat16
VMEM_LIMIT = 48 * 1024 * 1024


def normalize(values_in):
    widened = values_in.astype(F32)
    length = jnp.sqrt(jnp.sum(widened * widened, axis=-1, keepdims=True) + EPS)
    return (widened / length, length)


def project(unit_rows, length, grads):
    radial = jnp.sum(unit_rows * grads, axis=-1, keepdims=True)
    return (grads - unit_rows * radial) / length


def shifted(value, axis, steps):
    count = lax.axis_size(axis)
    return lax.ppermute(value, axis, [(i, (i + steps) % count) for i in range(count)])


def gathered(value, axis):
    return [value] + [shifted(value, axis, s) for s in (1, 2, 3)]


def returned(parts, axis):
    total = parts[0].astype(F32)
    for s in (1, 2, 3):
        total = total + shifted(parts[s], axis, -s).astype(F32)
    return total


def slopes_kernel(paired, *refs):
    images, texts = refs[0:4], refs[4:8]
    slopes_ref, parts, loss_ref = refs[8], refs[9:13], refs[13]
    img_all, txt_all = refs[14:16]
    own = images[0].shape[0]
    for s in range(4):
        img_all[pl.ds(s * own, own), :] = images[s][...]
        txt_all[pl.ds(s * own, own), :] = texts[s][...]
    logits = lax.dot_general(
        img_all[...], txt_all[...], (((1,), (1,)), ((), ())), preferred_element_type=F32
    )
    logits = logits * SCALE + SHIFT
    if paired:
        rows = lax.broadcasted_iota(jnp.int32, logits.shape, 0)
        cols = lax.broadcasted_iota(jnp.int32, logits.shape, 1)
        match = (rows == cols) & (rows < own)
        signed = jnp.where(match, -logits, logits)
    else:
        signed = logits
    small = jnp.exp(-jnp.abs(signed))
    losses = jnp.maximum(signed, 0.0) + jnp.log1p(small)
    sig = jnp.where(signed >= 0.0, 1.0, small) / (1.0 + small)
    slopes = sig * SCALE
    if paired:
        slopes = jnp.where(match, -slopes, slopes)
    low = slopes.astype(BF16)
    slopes_ref[...] = low
    width = losses.shape[1]
    lanes = losses[:, 0:128]
    for c in range(128, width - 127, 128):
        lanes = lanes + losses[:, c : c + 128]
    rest = width % 128
    loss_row = jnp.sum(lanes.T, axis=0, keepdims=True)
    if rest:
        loss_row = loss_row + jnp.sum(losses[:, width - rest :].T, axis=0, keepdims=True)
    loss_ref[...] = loss_row
    grads = lax.dot_general(
        low, img_all[...], (((0,), (0,)), ((), ())), preferred_element_type=F32
    ).astype(BF16)
    for s in range(4):
        parts[s][...] = grads[s * own : (s + 1) * own, :]


def slopes_call(paired, images, texts):
    own, features = images[0].shape
    rows = 4 * own
    unit = jax.ShapeDtypeStruct((own, features), BF16)
    out = pl.pallas_call(
        functools.partial(slopes_kernel, paired),
        out_shape=[jax.ShapeDtypeStruct((rows, rows), BF16)]
        + [unit] * 4
        + [jax.ShapeDtypeStruct((1, rows), F32)],
        in_specs=[pl.BlockSpec(memory_space=pltpu.VMEM)] * 8,
        out_specs=[pl.BlockSpec(memory_space=pltpu.VMEM)] * 6,
        scratch_shapes=[pltpu.VMEM((rows, features), BF16)] * 2,
        compiler_params=pltpu.CompilerParams(vmem_limit_bytes=VMEM_LIMIT),
        cost_estimate=pl.CostEstimate(
            flops=4 * rows * rows * features,
            bytes_accessed=12 * 2 * own * features + 2 * rows * rows,
            transcendentals=3 * rows * rows,
        ),
    )(*images, *texts)
    return out[0], out[1:5], out[5]


def image_kernel(*refs):
    first, second = refs[0:2]
    texts, later = refs[2:6], refs[6:10]
    parts = refs[10:14]
    txt_all = refs[14]
    own = texts[0].shape[0]
    for s in range(4):
        txt_all[pl.ds(s * own, own), :] = texts[s][...]
        txt_all[pl.ds((4 + s) * own, own), :] = later[s][...]
    half = 4 * own
    grads = jnp.dot(first[...], txt_all[0:half, :], preferred_element_type=F32)
    grads = grads + jnp.dot(second[...], txt_all[half:, :], preferred_element_type=F32)
    grads = grads.astype(BF16)
    for s in range(4):
        parts[s][...] = grads[s * own : (s + 1) * own, :]


def image_call(first, second, texts, later):
    own, features = texts[0].shape
    rows = 4 * own
    unit = jax.ShapeDtypeStruct((own, features), BF16)
    return pl.pallas_call(
        image_kernel,
        out_shape=[unit] * 4,
        in_specs=[pl.BlockSpec(memory_space=pltpu.VMEM)] * 10,
        out_specs=[pl.BlockSpec(memory_space=pltpu.VMEM)] * 4,
        scratch_shapes=[pltpu.VMEM((2 * rows, features), BF16)],
        compiler_params=pltpu.CompilerParams(vmem_limit_bytes=VMEM_LIMIT),
        cost_estimate=pl.CostEstimate(
            flops=4 * rows * rows * features,
            bytes_accessed=12 * 2 * own * features + 4 * rows * rows,
            transcendentals=0,
        ),
    )(first, second, *texts, *later)


def on_device(images, texts):
    img_unit, img_len = normalize(images)
    txt_unit, txt_len = normalize(texts)
    img_low, txt_low = img_unit.astype(BF16), txt_unit.astype(BF16)
    own = images.shape[0]
    moved = shifted(txt_low, BLK, 1)
    img_slots = gathered(img_low, "z")
    txt_slots = gathered(txt_low, "x")
    moved_slots = gathered(moved, "x")

    slopes0, parts0, loss0 = slopes_call(True, img_slots, txt_slots)
    slopes1, parts1, loss1 = slopes_call(False, img_slots, moved_slots)
    img_parts = image_call(slopes0, slopes1, txt_slots, moved_slots)

    home1 = shifted(returned(parts1, "x").astype(BF16), BLK, -1).astype(F32)
    img_grad = returned(img_parts, "z")
    txt_grad = returned(parts0, "x") + home1

    loss_slots = (loss0 + loss1).reshape(4, own)
    place = lax.axis_index("z")
    owner = lax.broadcasted_iota(jnp.int32, (NZ, own), 0)
    slot = lax.rem(place - owner + NZ, NZ)
    loss_at = jnp.zeros((NZ, own), F32)
    for s in range(4):
        loss_at = loss_at + jnp.where(slot == s, loss_slots[s][None, :], 0.0)
    row_loss = lax.psum_scatter(loss_at.reshape(-1), "z", scatter_dimension=0, tiled=True)

    image_grad = project(img_unit, img_len, img_grad)
    text_grad = project(txt_unit, txt_len, txt_grad)
    return (row_loss, image_grad, text_grad)


def solution(mesh):
    groups = mesh.devices.shape[0] // CORES
    fine = Mesh(mesh.devices.reshape(groups, CORES, NX, NZ), BLK + GRP)
    rows = P(BLK + GRP, None)
    return jax.shard_map(
        on_device,
        mesh=fine,
        in_specs=(rows, rows),
        out_specs=(P(BLK + GRP), rows, rows),
        check_vma=False,
    )
```

```python
import jax
import jax.numpy as jnp
from jax import lax
from jax.experimental import pallas as pl
from jax.experimental.pallas import tpu as pltpu
from jax.sharding import Mesh
from jax.sharding import PartitionSpec as P

SCALE = 10.0
SHIFT = -2.0
EPS = 1e-06
CORES, NX, NZ = 2, 4, 4
BLK, GRP = ("g", "core"), ("x", "z")
F32, BF16 = jnp.float32, jnp.bfloat16
MIB = 1024 * 1024
LOSS_ROWS = 16
CHUNK = 16
LANES = 128
WEIGHT = 60_000_000_000


def shifted(value, axis, steps):
    count = lax.axis_size(axis)
    return lax.ppermute(value, axis, [(i, (i + steps) % count) for i in range(count)])


def ring(value, steps):
    pairs = []
    for core in range(CORES):
        for x in range(NX):
            to = (x + (steps if core == 0 else -steps)) % NX
            pairs.append((core * NX + x, core * NX + to))
    return lax.ppermute(value, ("core", "x"), pairs)


def vmem_call(body, ins, outs, limit, scratch=(), flops=0, transcendentals=0, smem=0):
    size = sum(a.size * a.dtype.itemsize for a in list(ins) + list(outs))
    return pl.pallas_call(
        body,
        out_shape=list(outs),
        in_specs=[pl.BlockSpec(memory_space=pltpu.SMEM)] * smem
        + [pl.BlockSpec(memory_space=pltpu.VMEM)] * (len(ins) - smem),
        out_specs=[pl.BlockSpec(memory_space=pltpu.VMEM)] * len(outs),
        scratch_shapes=list(scratch),
        compiler_params=pltpu.CompilerParams(vmem_limit_bytes=limit * MIB),
        cost_estimate=pl.CostEstimate(
            flops=flops, bytes_accessed=size, transcendentals=transcendentals
        ),
    )(*ins)


def shape(dims, dtype):
    return jax.ShapeDtypeStruct(dims, dtype)


def unit_rows(values):
    wide = values.astype(F32)
    length = jnp.sqrt(jnp.sum(wide * wide, axis=-1, keepdims=True) + EPS)
    return wide / length, length


def low_kernel(img_ref, txt_ref, spread_ref, low_ref):
    unit, _ = unit_rows(txt_ref[...])
    low_ref[...] = unit.astype(BF16)
    unit, _ = unit_rows(img_ref[...])
    for z in range(NZ):
        spread_ref[z] = unit.astype(BF16)


def slopes_kernel(*refs):
    place_ref, img_all, texts = refs[0], refs[1], refs[2:6]
    slopes_ref, loss_ref, parts = refs[6], refs[7], refs[8:12]
    txt_all, scores, lanes_ref = refs[12:15]
    own = img_all.shape[0] // NZ
    pair = texts[0].shape[0]
    first = place_ref[0] * (own // CHUNK)
    for s in range(4):
        txt_all[pl.ds(s * pair, pair), :] = texts[s][...]
    scores[...] = lax.dot_general(
        img_all[...], txt_all[...], (((1,), (1,)), ((), ())), preferred_element_type=F32
    )
    width = scores.shape[1]

    def chunk(i, paired):
        rows = pl.ds(pl.multiple_of(i * CHUNK, CHUNK), CHUNK)
        logits = scores[rows, :] * SCALE + SHIFT
        if paired:
            row = lax.broadcasted_iota(jnp.int32, logits.shape, 0) + (i - first) * CHUNK
            col = lax.broadcasted_iota(jnp.int32, logits.shape, 1)
            match = row == col
            logits = jnp.where(match, -logits, logits)
        grown = jnp.exp(logits)
        losses = jnp.log1p(grown)
        slopes = SCALE * grown / (1.0 + grown)
        if paired:
            slopes = jnp.where(match, -slopes, slopes)
        slopes_ref[rows, :] = slopes.astype(BF16)
        total = losses[:, 0:LANES]
        for c in range(LANES, width, LANES):
            total = total + losses[:, c : c + LANES]
        lanes_ref[rows, :] = total

    @pl.loop(0, first)
    def _(i):
        chunk(i, False)

    @pl.loop(first, first + own // CHUNK)
    def _(i):
        chunk(i, True)

    @pl.loop(first + own // CHUNK, NZ * own // CHUNK)
    def _(i):
        chunk(i, False)

    loss_ref[...] = jnp.sum(lanes_ref[...].T, axis=0, keepdims=True)
    grads = lax.dot_general(
        slopes_ref[...], img_all[...], (((0,), (0,)), ((), ())), preferred_element_type=F32
    ).astype(BF16)
    for s in range(4):
        parts[s][...] = grads[s * pair : (s + 1) * pair, :]


def slopes_call(place, images, texts):
    rows, features = images.shape
    pair = texts[0].shape[0]
    cols = 4 * pair
    out = vmem_call(
        slopes_kernel,
        [place, images] + list(texts),
        [shape((rows, cols), BF16), shape((1, rows), F32)] + [shape((pair, features), BF16)] * 4,
        18,
        [
            pltpu.VMEM((cols, features), BF16),
            pltpu.VMEM((rows, cols), F32),
            pltpu.VMEM((rows, LANES), F32),
        ],
        flops=4 * rows * cols * features,
        transcendentals=3 * rows * cols,
        smem=1,
    )
    return out[0], out[1], out[2:6]


def image_kernel(*refs):
    slopes_ref, loss_ref = refs[0:2]
    texts, out_ref, txt_all = refs[2:6], refs[6], refs[7]
    pair = texts[0].shape[0]
    own = slopes_ref.shape[0] // 4
    for s in range(4):
        txt_all[pl.ds(s * pair, pair), :] = texts[s][...]
    grads = jnp.dot(slopes_ref[...], txt_all[...], preferred_element_type=F32).astype(BF16)
    row = lax.broadcasted_iota(jnp.int32, (LOSS_ROWS, own), 0)
    for s in range(4):
        out_ref[s, 0:own, :] = grads[s * own : (s + 1) * own, :]
        loss = loss_ref[:, s * own : (s + 1) * own]
        main = loss.astype(BF16).astype(F32)
        both = jnp.where(row == 0, main, jnp.where(row == 1, loss - main, 0.0))
        out_ref[s, own : own + LOSS_ROWS, :] = jnp.zeros((LOSS_ROWS, out_ref.shape[2]), BF16)
        out_ref[s, own : own + LOSS_ROWS, 0:own] = both.astype(BF16)


def image_call(slopes, loss, texts):
    pair, features = texts[0].shape
    rows, cols = slopes.shape
    (out,) = vmem_call(
        image_kernel,
        [slopes, loss] + list(texts),
        [shape((NZ, rows // NZ + LOSS_ROWS, features), BF16)],
        12,
        [pltpu.VMEM((cols, features), BF16)],
        flops=2 * rows * cols * features,
    )
    return out


def project(values, grads):
    unit, length = unit_rows(values)
    radial = jnp.sum(unit * grads, axis=-1, keepdims=True)
    return (grads - unit * radial) / length


def image_end_kernel(raw_ref, parts_ref, grad_ref, loss_ref):
    own = raw_ref.shape[0]
    grads = parts_ref[0, 0:own, :].astype(F32)
    tail = parts_ref[0, own : own + LOSS_ROWS, 0:own].astype(F32)
    for z in range(1, NZ):
        grads = grads + parts_ref[z, 0:own, :].astype(F32)
        tail = tail + parts_ref[z, own : own + LOSS_ROWS, 0:own].astype(F32)
    grad_ref[...] = project(raw_ref[...], grads)
    loss_ref[...] = jnp.sum(tail, axis=0, keepdims=True)


def text_end_kernel(raw_ref, a, b, c, home, grad_ref):
    own = raw_ref.shape[0]
    grads = a[0:own, :].astype(F32) + b[0:own, :].astype(F32)
    grads = grads + c[0:own, :].astype(F32) + home[...].astype(F32)
    grad_ref[...] = project(raw_ref[...], grads)


def later_kernel(a, b, c, out_ref):
    own = out_ref.shape[0]
    total = a[own:, :].astype(F32) + b[own:, :].astype(F32) + c[own:, :].astype(F32)
    out_ref[...] = total.astype(BF16)


def stack_kernel(a, b, out_ref):
    own = a.shape[0]
    out_ref[0:own, :] = a[...]
    out_ref[own:, :] = b[...]


def add_kernel(a, b, out_ref):
    out_ref[...] = (a[...].astype(F32) + b[...].astype(F32)).astype(BF16)


def on_device(images, texts):
    own, features = images.shape
    unit = shape((own, features), BF16)
    spread, txt_low = vmem_call(
        low_kernel, [images, texts], [shape((NZ, own, features), BF16), unit], 8
    )
    moved = shifted(txt_low, BLK, 1)
    img_all = lax.all_to_all(spread, "z", 0, 0).reshape(NZ * own, features)
    (both,) = vmem_call(
        stack_kernel, [txt_low, moved], [shape((2 * own, features), BF16)], 8, flops=WEIGHT
    )
    after, before = ring(both, 1), ring(both, -1)
    txt_slots = [both, after, before, ring(after, 1)]

    place = lax.axis_index("z").reshape(1).astype(jnp.int32)
    slopes, loss, txt_parts = slopes_call(place, img_all, txt_slots)
    far = ring(txt_parts[3], -1)
    img_parts = image_call(slopes, loss, txt_slots)
    img_back = lax.all_to_all(img_parts, "z", 0, 0)
    (joined,) = vmem_call(add_kernel, [txt_parts[1], far], [shape(far.shape, BF16)], 8, flops=WEIGHT)
    back1, back2 = ring(joined, -1), ring(txt_parts[2], 1)
    (later,) = vmem_call(later_kernel, [txt_parts[0], back1, back2], [unit], 8)
    home = shifted(later, BLK, -1)

    wide = shape((own, features), F32)
    image_grad, row_loss = vmem_call(
        image_end_kernel, [images, img_back], [wide, shape((1, own), F32)], 12
    )
    (text_grad,) = vmem_call(
        text_end_kernel, [texts, txt_parts[0], back1, back2, home], [wide], 12
    )
    return (row_loss.reshape(own), image_grad, text_grad)


def solution(mesh):
    groups = mesh.devices.shape[0] // CORES
    fine = Mesh(mesh.devices.reshape(groups, CORES, NX, NZ), BLK + GRP)
    rows = P(BLK + GRP, None)
    return jax.shard_map(
        on_device,
        mesh=fine,
        in_specs=(rows, rows),
        out_specs=(P(BLK + GRP), rows, rows),
        check_vma=False,
    )
```

```python
import functools

import jax
import jax.numpy as jnp
from jax import lax
from jax.experimental import pallas as pl
from jax.experimental.pallas import tpu as pltpu
from jax.sharding import Mesh
from jax.sharding import PartitionSpec as P

SCALE = 10.0
SHIFT = -2.0
EPS = 1e-06
CORES, NX, NZ = 2, 4, 4
BLK, GRP = ("g", "core"), ("x", "z")
F32, BF16 = jnp.float32, jnp.bfloat16
MIB = 1024 * 1024
LOSS_ROWS = 16
CHUNK = 16
LANES = 128
WEIGHT = 60_000_000_000


def shifted(value, axis, steps):
    count = lax.axis_size(axis)
    return lax.ppermute(value, axis, [(i, (i + steps) % count) for i in range(count)])


def vmem_call(body, ins, outs, limit, scratch=(), flops=0, transcendentals=0, smem=0):
    size = sum(a.size * a.dtype.itemsize for a in list(ins) + list(outs))
    return pl.pallas_call(
        body,
        out_shape=list(outs),
        in_specs=[pl.BlockSpec(memory_space=pltpu.SMEM)] * smem
        + [pl.BlockSpec(memory_space=pltpu.VMEM)] * (len(ins) - smem),
        out_specs=[pl.BlockSpec(memory_space=pltpu.VMEM)] * len(outs),
        scratch_shapes=list(scratch),
        compiler_params=pltpu.CompilerParams(vmem_limit_bytes=limit * MIB),
        cost_estimate=pl.CostEstimate(
            flops=flops, bytes_accessed=size, transcendentals=transcendentals
        ),
    )(*ins)


def shape(dims, dtype):
    return jax.ShapeDtypeStruct(dims, dtype)


def unit_rows(values):
    wide = values.astype(F32)
    length = jnp.sqrt(jnp.sum(wide * wide, axis=-1, keepdims=True) + EPS)
    return wide / length, length


def low_kernel(img_ref, txt_ref, spread_ref, low_ref):
    unit, _ = unit_rows(img_ref[...])
    for z in range(NZ):
        spread_ref[z] = unit.astype(BF16)
    unit, _ = unit_rows(txt_ref[...])
    low_ref[...] = unit.astype(BF16)


def moved_kernel(txt_ref, low_ref):
    unit, _ = unit_rows(txt_ref[...])
    low_ref[...] = unit.astype(BF16)


def slopes_kernel(*refs):
    place_ref, img_all, texts = refs[0], refs[1], refs[2:10]
    slopes_ref, out_ref = refs[10:12]
    txt_all, scores, lanes_ref = refs[12:15]
    own = img_all.shape[0] // NZ
    first = place_ref[0] * (own // CHUNK)
    for s in range(8):
        txt_all[pl.ds(s * own, own), :] = texts[s][...]
    scores[...] = lax.dot_general(
        img_all[...], txt_all[...], (((1,), (1,)), ((), ())), preferred_element_type=F32
    )
    width = scores.shape[1]

    def chunk(i, paired):
        rows = pl.ds(pl.multiple_of(i * CHUNK, CHUNK), CHUNK)
        logits = scores[rows, :] * SCALE + SHIFT
        if paired:
            row = lax.broadcasted_iota(jnp.int32, logits.shape, 0) + (i - first) * CHUNK
            col = lax.broadcasted_iota(jnp.int32, logits.shape, 1)
            match = row == col
            logits = jnp.where(match, -logits, logits)
        grown = jnp.exp(logits)
        losses = jnp.log1p(grown)
        slopes = SCALE * grown / (1.0 + grown)
        if paired:
            slopes = jnp.where(match, -slopes, slopes)
        slopes_ref[rows, :] = slopes.astype(BF16)
        total = losses[:, 0:LANES]
        for c in range(LANES, width, LANES):
            total = total + losses[:, c : c + LANES]
        lanes_ref[rows, :] = total

    @pl.loop(0, first)
    def _(i):
        chunk(i, False)

    @pl.loop(first, first + own // CHUNK)
    def _(i):
        chunk(i, True)

    @pl.loop(first + own // CHUNK, NZ * own // CHUNK)
    def _(i):
        chunk(i, False)

    loss_row = jnp.sum(lanes_ref[...].T, axis=0, keepdims=True)
    grads = jnp.dot(slopes_ref[...], txt_all[...], preferred_element_type=F32).astype(BF16)
    row = lax.broadcasted_iota(jnp.int32, (LOSS_ROWS, own), 0)
    for s in range(NZ):
        out_ref[s, 0:own, :] = grads[s * own : (s + 1) * own, :]
        loss = loss_row[:, s * own : (s + 1) * own]
        main = loss.astype(BF16).astype(F32)
        both = jnp.where(row == 0, main, jnp.where(row == 1, loss - main, 0.0))
        out_ref[s, own : own + LOSS_ROWS, :] = jnp.zeros((LOSS_ROWS, out_ref.shape[2]), BF16)
        out_ref[s, own : own + LOSS_ROWS, 0:own] = both.astype(BF16)


def slopes_call(place, images, texts):
    rows, features = images.shape
    own = rows // NZ
    cols = len(texts) * own
    return vmem_call(
        slopes_kernel,
        [place, images] + list(texts),
        [shape((rows, cols), BF16), shape((NZ, own + LOSS_ROWS, features), BF16)],
        18,
        [
            pltpu.VMEM((cols, features), BF16),
            pltpu.VMEM((rows, cols), F32),
            pltpu.VMEM((rows, LANES), F32),
        ],
        flops=4 * rows * cols * features,
        transcendentals=3 * rows * cols,
        smem=1,
    )


def text_kernel(base, slopes_ref, img_all, *parts):
    own = parts[0].shape[0]
    cols = len(parts) * own
    wide = slopes_ref.shape[1]
    start = base * cols // LANES * LANES
    grads = lax.dot_general(
        slopes_ref[:, start : wide if base else -(-cols // LANES) * LANES],
        img_all[...],
        (((0,), (0,)), ((), ())),
        preferred_element_type=F32,
    ).astype(BF16)
    skip = base * cols - start
    for s, part in enumerate(parts):
        part[...] = grads[skip + s * own : skip + (s + 1) * own, :]


def text_call(base, slopes, images):
    rows, features = images.shape
    own = rows // NZ
    return vmem_call(
        functools.partial(text_kernel, base),
        [slopes, images],
        [shape((own, features), BF16)] * NX,
        12,
        flops=2 * rows * NX * own * features,
    )


def project(values, grads):
    unit, length = unit_rows(values)
    radial = jnp.sum(unit * grads, axis=-1, keepdims=True)
    return (grads - unit * radial) / length


def image_end_kernel(raw_ref, parts_ref, grad_ref, loss_ref):
    own = raw_ref.shape[0]
    grads = parts_ref[0, 0:own, :].astype(F32)
    tail = parts_ref[0, own : own + LOSS_ROWS, 0:own].astype(F32)
    for z in range(1, NZ):
        grads = grads + parts_ref[z, 0:own, :].astype(F32)
        tail = tail + parts_ref[z, own : own + LOSS_ROWS, 0:own].astype(F32)
    grad_ref[...] = project(raw_ref[...], grads)
    loss_ref[...] = jnp.sum(tail, axis=0, keepdims=True)


def text_end_kernel(raw_ref, a, b, c, d, home, grad_ref):
    grads = a[...].astype(F32) + b[...].astype(F32)
    grads = grads + c[...].astype(F32) + d[...].astype(F32)
    grads = grads + home[...].astype(F32)
    grad_ref[...] = project(raw_ref[...], grads)


def later_kernel(a, b, c, d, out_ref):
    total = a[...].astype(F32) + b[...].astype(F32)
    total = total + c[...].astype(F32) + d[...].astype(F32)
    out_ref[...] = total.astype(BF16)


def spread_x(value):
    return [value] + [shifted(value, "x", s) for s in (2, 1, 3)]


def return_x(parts):
    return [parts[0]] + [shifted(p, "x", -s) for p, s in zip(parts[1:], (2, 1, 3))]


def on_device(images, texts):
    own, features = images.shape
    unit = shape((own, features), BF16)
    moved = shifted(texts, BLK, 1)
    spread, txt_low = vmem_call(
        low_kernel, [images, texts], [shape((NZ, own, features), BF16), unit], 8
    )
    img_all = lax.all_to_all(spread, "z", 0, 0).reshape(NZ * own, features)
    now_slots = spread_x(txt_low)
    (moved_low,) = vmem_call(moved_kernel, [moved], [unit], 8, flops=WEIGHT)
    later_slots = spread_x(moved_low)

    place = lax.axis_index("z").reshape(1).astype(jnp.int32)
    slopes, img_parts = slopes_call(place, img_all, now_slots + later_slots)
    img_back = lax.all_to_all(img_parts, "z", 0, 0)
    later_back = return_x(text_call(1, slopes, img_all))
    (later,) = vmem_call(later_kernel, later_back, [unit], 8)
    home = shifted(later, BLK, -1)
    now_back = return_x(text_call(0, slopes, img_all))

    wide = shape((own, features), F32)
    image_grad, row_loss = vmem_call(
        image_end_kernel, [images, img_back], [wide, shape((1, own), F32)], 12
    )
    (text_grad,) = vmem_call(text_end_kernel, [texts] + now_back + [home], [wide], 12)
    return (row_loss.reshape(own), image_grad, text_grad)


def solution(mesh):
    groups = mesh.devices.shape[0] // CORES
    fine = Mesh(mesh.devices.reshape(groups, CORES, NX, NZ), BLK + GRP)
    rows = P(BLK + GRP, None)
    return jax.shard_map(
        on_device,
        mesh=fine,
        in_specs=(rows, rows),
        out_specs=(P(BLK + GRP), rows, rows),
        check_vma=False,
    )
```

```python
import functools

import jax
import jax.numpy as jnp
from jax import lax
from jax.experimental import pallas as pl
from jax.experimental.pallas import tpu as pltpu
from jax.sharding import Mesh
from jax.sharding import PartitionSpec as P

SCALE = 10.0
SHIFT = -2.0
EPS = 1e-06
CORES, NX, NZ = 2, 4, 4
BLK, GRP = ("g", "core"), ("x", "z")
F32, BF16 = jnp.float32, jnp.bfloat16
MIB = 1024 * 1024
LOSS_ROWS = 16
CHUNK = 16
LANES = 128
WEIGHT = 26_000_000_000
HOME_WEIGHT = 4_000_000_000


def shifted(value, axis, steps):
    count = lax.axis_size(axis)
    return lax.ppermute(value, axis, [(i, (i + steps) % count) for i in range(count)])


def vmem_call(body, ins, outs, limit, scratch=(), flops=0, transcendentals=0, smem=0):
    size = sum(a.size * a.dtype.itemsize for a in list(ins) + list(outs))
    return pl.pallas_call(
        body,
        out_shape=list(outs),
        in_specs=[pl.BlockSpec(memory_space=pltpu.SMEM)] * smem
        + [pl.BlockSpec(memory_space=pltpu.VMEM)] * (len(ins) - smem),
        out_specs=[pl.BlockSpec(memory_space=pltpu.VMEM)] * len(outs),
        scratch_shapes=list(scratch),
        compiler_params=pltpu.CompilerParams(vmem_limit_bytes=limit * MIB),
        cost_estimate=pl.CostEstimate(
            flops=flops, bytes_accessed=size, transcendentals=transcendentals
        ),
    )(*ins)


def shape(dims, dtype):
    return jax.ShapeDtypeStruct(dims, dtype)


def unit_rows(values):
    wide = values.astype(F32)
    length = jnp.sqrt(jnp.sum(wide * wide, axis=-1, keepdims=True) + EPS)
    return wide / length, length


def low_kernel(img_ref, txt_ref, spread_ref, low_ref):
    unit, _ = unit_rows(img_ref[...])
    for z in range(NZ):
        spread_ref[z] = unit.astype(BF16)
    unit, _ = unit_rows(txt_ref[...])
    low_ref[...] = unit.astype(BF16)


def moved_kernel(txt_ref, low_ref):
    unit, _ = unit_rows(txt_ref[...])
    low_ref[...] = unit.astype(BF16)


def slopes_kernel(*refs):
    place_ref, img_all, texts = refs[0], refs[1], refs[2:10]
    slopes_ref, out_ref = refs[10:12]
    txt_all, scores, lanes_ref = refs[12:15]
    own = img_all.shape[0] // NZ
    first = place_ref[0] * (own // CHUNK)
    for s in range(8):
        txt_all[pl.ds(s * own, own), :] = texts[s][...]
    scores[...] = lax.dot_general(
        img_all[...], txt_all[...], (((1,), (1,)), ((), ())), preferred_element_type=F32
    )
    width = scores.shape[1]

    def chunk(i, paired):
        rows = pl.ds(pl.multiple_of(i * CHUNK, CHUNK), CHUNK)
        logits = scores[rows, :] * SCALE + SHIFT
        if paired:
            row = lax.broadcasted_iota(jnp.int32, logits.shape, 0) + (i - first) * CHUNK
            col = lax.broadcasted_iota(jnp.int32, logits.shape, 1)
            match = row == col
            logits = jnp.where(match, -logits, logits)
        grown = jnp.exp(logits)
        losses = jnp.log1p(grown)
        slopes = SCALE * grown / (1.0 + grown)
        if paired:
            slopes = jnp.where(match, -slopes, slopes)
        slopes_ref[rows, :] = slopes.astype(BF16)
        total = losses[:, 0:LANES]
        for c in range(LANES, width, LANES):
            total = total + losses[:, c : c + LANES]
        lanes_ref[rows, :] = total

    @pl.loop(0, first)
    def _(i):
        chunk(i, False)

    @pl.loop(first, first + own // CHUNK)
    def _(i):
        chunk(i, True)

    @pl.loop(first + own // CHUNK, NZ * own // CHUNK)
    def _(i):
        chunk(i, False)

    loss_row = jnp.sum(lanes_ref[...].T, axis=0, keepdims=True)
    grads = jnp.dot(slopes_ref[...], txt_all[...], preferred_element_type=F32).astype(BF16)
    row = lax.broadcasted_iota(jnp.int32, (LOSS_ROWS, own), 0)
    for s in range(NZ):
        out_ref[s, 0:own, :] = grads[s * own : (s + 1) * own, :]
        loss = loss_row[:, s * own : (s + 1) * own]
        main = loss.astype(BF16).astype(F32)
        both = jnp.where(row == 0, main, jnp.where(row == 1, loss - main, 0.0))
        out_ref[s, own : own + LOSS_ROWS, :] = jnp.zeros((LOSS_ROWS, out_ref.shape[2]), BF16)
        out_ref[s, own : own + LOSS_ROWS, 0:own] = both.astype(BF16)


def slopes_call(place, images, texts):
    rows, features = images.shape
    own = rows // NZ
    cols = len(texts) * own
    return vmem_call(
        slopes_kernel,
        [place, images] + list(texts),
        [shape((rows, cols), BF16), shape((NZ, own + LOSS_ROWS, features), BF16)],
        18,
        [
            pltpu.VMEM((cols, features), BF16),
            pltpu.VMEM((rows, cols), F32),
            pltpu.VMEM((rows, LANES), F32),
        ],
        flops=4 * rows * cols * features,
        transcendentals=3 * rows * cols,
        smem=1,
    )


def text_kernel(base, slopes_ref, img_all, *parts):
    own = parts[0].shape[0]
    cols = len(parts) * own
    wide = slopes_ref.shape[1]
    start = base * cols // LANES * LANES
    grads = lax.dot_general(
        slopes_ref[:, start : wide if base else -(-cols // LANES) * LANES],
        img_all[...],
        (((0,), (0,)), ((), ())),
        preferred_element_type=F32,
    ).astype(BF16)
    skip = base * cols - start
    for s, part in enumerate(parts):
        part[...] = grads[skip + s * own : skip + (s + 1) * own, :]


def text_call(base, slopes, images):
    rows, features = images.shape
    own = rows // NZ
    return vmem_call(
        functools.partial(text_kernel, base),
        [slopes, images],
        [shape((own, features), BF16)] * NX,
        12,
        flops=2 * rows * NX * own * features,
    )


def project(values, grads):
    unit, length = unit_rows(values)
    radial = jnp.sum(unit * grads, axis=-1, keepdims=True)
    return (grads - unit * radial) / length


def image_end_kernel(raw_ref, parts_ref, grad_ref, loss_ref):
    own = raw_ref.shape[0]
    grads = parts_ref[0, 0:own, :].astype(F32)
    tail = parts_ref[0, own : own + LOSS_ROWS, 0:own].astype(F32)
    for z in range(1, NZ):
        grads = grads + parts_ref[z, 0:own, :].astype(F32)
        tail = tail + parts_ref[z, own : own + LOSS_ROWS, 0:own].astype(F32)
    grad_ref[...] = project(raw_ref[...], grads)
    loss_ref[...] = jnp.sum(tail, axis=0, keepdims=True)


def text_end_kernel(raw_ref, base, b, c, d, grad_ref):
    grads = base[...] + b[...].astype(F32)
    grads = grads + c[...].astype(F32) + d[...].astype(F32)
    grad_ref[...] = project(raw_ref[...], grads)


def base_kernel(a, home, out_ref):
    out_ref[...] = a[...].astype(F32) + home[...].astype(F32)


def later_kernel(a, b, c, d, out_ref):
    total = a[...].astype(F32) + b[...].astype(F32)
    total = total + c[...].astype(F32) + d[...].astype(F32)
    out_ref[...] = total.astype(BF16)


def spread_x(value):
    return [value] + [shifted(value, "x", s) for s in (2, 1, 3)]


def return_x(parts):
    return [parts[0]] + [shifted(p, "x", -s) for p, s in zip(parts[1:], (2, 1, 3))]


def on_device(images, texts):
    own, features = images.shape
    unit = shape((own, features), BF16)
    moved = shifted(texts, BLK, 1)
    spread, txt_low = vmem_call(
        low_kernel, [images, texts], [shape((NZ, own, features), BF16), unit], 8
    )
    img_all = lax.all_to_all(spread, "z", 0, 0).reshape(NZ * own, features)
    now_slots = spread_x(txt_low)
    (moved_low,) = vmem_call(moved_kernel, [moved], [unit], 8, flops=WEIGHT)
    later_slots = spread_x(moved_low)

    place = lax.axis_index("z").reshape(1).astype(jnp.int32)
    slopes, img_parts = slopes_call(place, img_all, now_slots + later_slots)
    img_back = lax.all_to_all(img_parts, "z", 0, 0)
    later_back = return_x(text_call(1, slopes, img_all))
    (later,) = vmem_call(later_kernel, later_back, [unit], 8)
    home = shifted(later, BLK, -1)
    now_back = return_x(text_call(0, slopes, img_all))

    wide = shape((own, features), F32)
    image_grad, row_loss = vmem_call(
        image_end_kernel, [images, img_back], [wide, shape((1, own), F32)], 12
    )
    (base,) = vmem_call(base_kernel, [now_back[0], home], [wide], 8, flops=HOME_WEIGHT)
    (text_grad,) = vmem_call(text_end_kernel, [texts, base] + now_back[1:], [wide], 12)
    return (row_loss.reshape(own), image_grad, text_grad)


def solution(mesh):
    groups = mesh.devices.shape[0] // CORES
    fine = Mesh(mesh.devices.reshape(groups, CORES, NX, NZ), BLK + GRP)
    rows = P(BLK + GRP, None)
    return jax.shard_map(
        on_device,
        mesh=fine,
        in_specs=(rows, rows),
        out_specs=(P(BLK + GRP), rows, rows),
        check_vma=False,
    )
```

```python
import jax
import jax.numpy as jnp
from jax import lax
from jax.experimental import pallas as pl
from jax.experimental.pallas import tpu as pltpu
from jax.sharding import Mesh
from jax.sharding import PartitionSpec as P

SCALE = 10.0
SHIFT = -2.0
EPS = 1e-06
CORES, NX, NZ = 2, 4, 4
BLK, GRP = ("g", "core"), ("x", "z")
F32, BF16 = jnp.float32, jnp.bfloat16
MIB = 1024 * 1024
LOSS_ROWS = 16
CHUNK = 16
LANES = 128
HOPS = (2, 1, 3)
WEIGHT = 26_000_000_000
HOME_WEIGHT = 4_000_000_000
FAR_WEIGHT = 10_000_000_000


def shifted(value, axis, steps):
    count = lax.axis_size(axis)
    return lax.ppermute(value, axis, [(i, (i + steps) % count) for i in range(count)])


def across_z(value, bit):
    return lax.ppermute(value, "z", [(z, z ^ bit) for z in range(NZ)])


def next_group(value, back):
    count = lax.axis_size("g")
    pairs = [(2 * g + 1, 2 * ((g + 1) % count)) for g in range(count)]
    if back:
        pairs = [(b, a) for a, b in pairs]
    return lax.ppermute(value, BLK, pairs)


def first_core(value, steps):
    return lax.ppermute(value, ("core", "x"), [(x, (x + steps) % NX) for x in range(NX)])


def vmem_call(body, ins, outs, limit, scratch=(), flops=0, transcendentals=0, smem=0):
    size = sum(a.size * a.dtype.itemsize for a in list(ins) + list(outs))
    return pl.pallas_call(
        body,
        out_shape=list(outs),
        in_specs=[pl.BlockSpec(memory_space=pltpu.SMEM)] * smem
        + [pl.BlockSpec(memory_space=pltpu.VMEM)] * (len(ins) - smem),
        out_specs=[pl.BlockSpec(memory_space=pltpu.VMEM)] * len(outs),
        scratch_shapes=list(scratch),
        compiler_params=pltpu.CompilerParams(vmem_limit_bytes=limit * MIB),
        cost_estimate=pl.CostEstimate(
            flops=flops, bytes_accessed=size, transcendentals=transcendentals
        ),
    )(*ins)


def shape(dims, dtype):
    return jax.ShapeDtypeStruct(dims, dtype)


def unit_rows(values):
    wide = values.astype(F32)
    length = jnp.sqrt(jnp.sum(wide * wide, axis=-1, keepdims=True) + EPS)
    return wide / length, length


def low_kernel(img_ref, txt_ref, spread_ref, low_ref):
    unit, _ = unit_rows(img_ref[...])
    for z in range(NZ):
        spread_ref[z] = unit.astype(BF16)
    unit, _ = unit_rows(txt_ref[...])
    low_ref[...] = unit.astype(BF16)


def moved_kernel(txt_ref, low_ref):
    unit, _ = unit_rows(txt_ref[...])
    low_ref[...] = unit.astype(BF16)


def slopes_kernel(*refs):
    place_ref, img_all, texts = refs[0], refs[1], refs[2:10]
    slopes_ref, keep, send = refs[10:13]
    txt_all, scores, lanes_ref, low, tails = refs[13:18]
    own = img_all.shape[0] // NZ
    first = place_ref[0] * (own // CHUNK)
    for s in range(8):
        txt_all[pl.ds(s * own, own), :] = texts[s][...]
    scores[...] = lax.dot_general(
        img_all[...], txt_all[...], (((1,), (1,)), ((), ())), preferred_element_type=F32
    )
    width = scores.shape[1]

    def chunk(i, paired):
        rows = pl.ds(pl.multiple_of(i * CHUNK, CHUNK), CHUNK)
        logits = scores[rows, :] * SCALE + SHIFT
        if paired:
            row = lax.broadcasted_iota(jnp.int32, logits.shape, 0) + (i - first) * CHUNK
            col = lax.broadcasted_iota(jnp.int32, logits.shape, 1)
            match = row == col
            logits = jnp.where(match, -logits, logits)
        grown = jnp.exp(logits)
        losses = jnp.log1p(grown)
        slopes = SCALE * grown / (1.0 + grown)
        if paired:
            slopes = jnp.where(match, -slopes, slopes)
        slopes_ref[rows, :] = slopes.astype(BF16)
        total = losses[:, 0:LANES]
        for c in range(LANES, width, LANES):
            total = total + losses[:, c : c + LANES]
        lanes_ref[rows, :] = total

    @pl.loop(0, first)
    def _(i):
        chunk(i, False)

    @pl.loop(first, first + own // CHUNK)
    def _(i):
        chunk(i, True)

    @pl.loop(first + own // CHUNK, NZ * own // CHUNK)
    def _(i):
        chunk(i, False)

    loss_row = jnp.sum(lanes_ref[...].T, axis=0, keepdims=True)
    low[...] = jnp.dot(slopes_ref[...], txt_all[...], preferred_element_type=F32).astype(BF16)
    row = lax.broadcasted_iota(jnp.int32, (LOSS_ROWS, own), 0)
    tails[...] = jnp.zeros(tails.shape, BF16)
    for z in range(NZ):
        loss = loss_row[:, z * own : (z + 1) * own]
        main = loss.astype(BF16).astype(F32)
        both = jnp.where(row == 0, main, jnp.where(row == 1, loss - main, 0.0))
        tails[z, :, 0:own] = both.astype(BF16)
    tall = own + LOSS_ROWS
    for s, bits in enumerate((0, 2, 1, 3)):
        z = place_ref[0] ^ bits
        out_ref = keep if s < 2 else send
        at = s % 2 * tall
        out_ref[at : at + own, :] = low[pl.ds(pl.multiple_of(z * own, CHUNK), own), :]
        out_ref[at + own : at + tall, :] = tails[z]


def slopes_call(place, images, texts):
    rows, features = images.shape
    own = rows // NZ
    cols = len(texts) * own
    return vmem_call(
        slopes_kernel,
        [place, images] + list(texts),
        [shape((rows, cols), BF16)] + [shape((2 * (own + LOSS_ROWS), features), BF16)] * 2,
        18,
        [
            pltpu.VMEM((cols, features), BF16),
            pltpu.VMEM((rows, cols), F32),
            pltpu.VMEM((rows, LANES), F32),
            pltpu.VMEM((rows, features), BF16),
            pltpu.VMEM((NZ, LOSS_ROWS, features), BF16),
        ],
        flops=4 * rows * cols * features,
        transcendentals=3 * rows * cols,
        smem=1,
    )


def text_grads(slopes, images):
    return lax.dot_general(
        slopes, images, (((0,), (0,)), ((), ())), preferred_element_type=F32
    )


def later_parts_kernel(slopes_ref, img_all, stack, *parts):
    own = parts[0].shape[0]
    cols = stack.shape[0]
    start = cols // LANES * LANES
    grads = text_grads(slopes_ref[:, start:], img_all[...]).astype(BF16)
    stack[...] = grads[cols - start :, :]
    for s, part in enumerate(parts):
        at = cols - start + s * own
        part[...] = grads[at : at + own, :]


def now_parts_kernel(slopes_ref, img_all, other, *parts):
    own = parts[0].shape[0]
    cols = other.shape[0]
    grads = text_grads(slopes_ref[:, 0 : -(-cols // LANES) * LANES], img_all[...])
    grads = (grads[0:cols, :] + other[...].astype(F32)).astype(BF16)
    for s, part in enumerate(parts):
        part[...] = grads[s * own : (s + 1) * own, :]


def text_call(body, ins, outs):
    flops = 2 * ins[0].shape[0] * ins[0].shape[1] * ins[1].shape[1] // 2
    return vmem_call(body, ins, outs, 12, flops=flops)


def project(values, grads):
    unit, length = unit_rows(values)
    radial = jnp.sum(unit * grads, axis=-1, keepdims=True)
    return (grads - unit * radial) / length


def far_kernel(mine, theirs, out_ref):
    tall = out_ref.shape[0]
    out_ref[...] = (mine[tall:, :].astype(F32) + theirs[tall:, :].astype(F32)).astype(BF16)


def image_end_kernel(raw_ref, mine, near, far, grad_ref, loss_ref):
    own = raw_ref.shape[0]
    grads = jnp.zeros(raw_ref.shape, F32)
    tail = jnp.zeros((LOSS_ROWS, own), F32)
    for part in (mine, near, far):
        grads = grads + part[0:own, :].astype(F32)
        tail = tail + part[own : own + LOSS_ROWS, 0:own].astype(F32)
    grad_ref[...] = project(raw_ref[...], grads)
    loss_ref[...] = jnp.sum(tail, axis=0, keepdims=True)


def text_end_kernel(raw_ref, base, b, c, d, grad_ref):
    grads = base[...] + b[...].astype(F32)
    grads = grads + c[...].astype(F32) + d[...].astype(F32)
    grad_ref[...] = project(raw_ref[...], grads)


def base_kernel(a, home, out_ref):
    out_ref[...] = a[...].astype(F32) + home[...].astype(F32)


def later_kernel(a, b, c, d, out_ref):
    total = a[...].astype(F32) + b[...].astype(F32)
    total = total + c[...].astype(F32) + d[...].astype(F32)
    out_ref[...] = total.astype(BF16)


def spread_x(value):
    return [value] + [shifted(value, "x", s) for s in HOPS]


def on_device(images, texts):
    own, features = images.shape
    unit = shape((own, features), BF16)
    moved = shifted(texts, BLK, 1)
    spread, txt_low = vmem_call(
        low_kernel, [images, texts], [shape((NZ, own, features), BF16), unit], 8
    )
    img_all = lax.all_to_all(spread, "z", 0, 0).reshape(NZ * own, features)
    now_slots = spread_x(txt_low)
    (moved_low,) = vmem_call(moved_kernel, [moved], [unit], 8, flops=WEIGHT)
    later_slots = spread_x(moved_low)

    place = lax.axis_index("z").reshape(1).astype(jnp.int32)
    slopes, keep, send = slopes_call(place, img_all, now_slots + later_slots)
    back_near = across_z(send, 1)
    tall = shape((own + LOSS_ROWS, features), BF16)
    (far_send,) = vmem_call(far_kernel, [keep, back_near], [tall], 8, flops=FAR_WEIGHT)
    back_far = across_z(far_send, 2)
    all_x = shape((NX * own, features), BF16)
    out = text_call(later_parts_kernel, [slopes, img_all], [all_x] + [unit] * NX)
    across = lax.ppermute(out[0], "core", [(1, 0)])
    later_back = [out[1]] + [first_core(p, -s) for p, s in zip(out[2:], HOPS)]
    (later,) = vmem_call(later_kernel, later_back, [unit], 8)
    home = next_group(later, True)
    parts = text_call(now_parts_kernel, [slopes, img_all, across], [unit] * NX)
    now_back = [parts[0]] + [shifted(p, "x", -s) for p, s in zip(parts[1:], HOPS)]

    back_far, home, now_back = lax.optimization_barrier((back_far, home, now_back))
    wide = shape((own, features), F32)
    image_grad, row_loss = vmem_call(
        image_end_kernel, [images, keep, back_near, back_far], [wide, shape((1, own), F32)], 12
    )
    (base,) = vmem_call(base_kernel, [now_back[0], home], [wide], 8, flops=HOME_WEIGHT)
    (text_grad,) = vmem_call(text_end_kernel, [texts, base] + now_back[1:], [wide], 12)
    return (row_loss.reshape(own), image_grad, text_grad)


def solution(mesh):
    groups = mesh.devices.shape[0] // CORES
    fine = Mesh(mesh.devices.reshape(groups, CORES, NX, NZ), BLK + GRP)
    rows = P(BLK + GRP, None)
    return jax.shard_map(
        on_device,
        mesh=fine,
        in_specs=(rows, rows),
        out_specs=(P(BLK + GRP), rows, rows),
        check_vma=False,
    )
```

```python
import jax
import jax.numpy as jnp
from jax import lax
from jax.experimental import pallas as pl
from jax.experimental.pallas import tpu as pltpu
from jax.sharding import Mesh
from jax.sharding import PartitionSpec as P

SCALE = 10.0
SHIFT = -2.0
EPS = 1e-06
CORES, NX, NZ = 2, 4, 4
BLK, GRP = ("g", "core"), ("x", "z")
F32, BF16 = jnp.float32, jnp.bfloat16
MIB = 1024 * 1024
LOSS_ROWS = 16
CHUNK = 16
LANES = 128
HOPS = (2, 1, 3)
WEIGHT = 26_000_000_000
HOME_WEIGHT = 4_000_000_000
FAR_WEIGHT = 10_000_000_000


def shifted(value, axis, steps):
    count = lax.axis_size(axis)
    return lax.ppermute(value, axis, [(i, (i + steps) % count) for i in range(count)])


def across_z(value, step):
    pairs = []
    for core in range(CORES):
        bit = 1 if step == core else 2
        pairs += [(core * NZ + z, core * NZ + (z ^ bit)) for z in range(NZ)]
    return lax.ppermute(value, ("core", "z"), pairs)


def next_group(value, back):
    count = lax.axis_size("g")
    pairs = [(2 * g + 1, 2 * ((g + 1) % count)) for g in range(count)]
    if back:
        pairs = [(b, a) for a, b in pairs]
    return lax.ppermute(value, BLK, pairs)


def first_core(value, steps):
    return lax.ppermute(value, ("core", "x"), [(x, (x + steps) % NX) for x in range(NX)])


def vmem_call(body, ins, outs, limit, scratch=(), flops=0, transcendentals=0, smem=0):
    size = sum(a.size * a.dtype.itemsize for a in list(ins) + list(outs))
    return pl.pallas_call(
        body,
        out_shape=list(outs),
        in_specs=[pl.BlockSpec(memory_space=pltpu.SMEM)] * smem
        + [pl.BlockSpec(memory_space=pltpu.VMEM)] * (len(ins) - smem),
        out_specs=[pl.BlockSpec(memory_space=pltpu.VMEM)] * len(outs),
        scratch_shapes=list(scratch),
        compiler_params=pltpu.CompilerParams(vmem_limit_bytes=limit * MIB),
        cost_estimate=pl.CostEstimate(
            flops=flops, bytes_accessed=size, transcendentals=transcendentals
        ),
    )(*ins)


def shape(dims, dtype):
    return jax.ShapeDtypeStruct(dims, dtype)


def unit_rows(values):
    wide = values.astype(F32)
    length = jnp.sqrt(jnp.sum(wide * wide, axis=-1, keepdims=True) + EPS)
    return wide / length, length


def low_kernel(img_ref, txt_ref, spread_ref, low_ref):
    unit, _ = unit_rows(img_ref[...])
    for z in range(NZ):
        spread_ref[z] = unit.astype(BF16)
    unit, _ = unit_rows(txt_ref[...])
    low_ref[...] = unit.astype(BF16)


def moved_kernel(txt_ref, low_ref):
    unit, _ = unit_rows(txt_ref[...])
    low_ref[...] = unit.astype(BF16)


def slopes_kernel(*refs):
    place_ref, img_all, texts = refs[0], refs[1], refs[2:10]
    slopes_ref, keep, send = refs[10:13]
    txt_all, scores, lanes_ref, low, tails = refs[13:18]
    own = img_all.shape[0] // NZ
    first = place_ref[0] * (own // CHUNK)
    for s in range(8):
        txt_all[pl.ds(s * own, own), :] = texts[s][...]
    scores[...] = lax.dot_general(
        img_all[...], txt_all[...], (((1,), (1,)), ((), ())), preferred_element_type=F32
    )
    width = scores.shape[1]

    def chunk(i, paired):
        rows = pl.ds(pl.multiple_of(i * CHUNK, CHUNK), CHUNK)
        logits = scores[rows, :] * SCALE + SHIFT
        if paired:
            row = lax.broadcasted_iota(jnp.int32, logits.shape, 0) + (i - first) * CHUNK
            col = lax.broadcasted_iota(jnp.int32, logits.shape, 1)
            match = row == col
            logits = jnp.where(match, -logits, logits)
        grown = jnp.exp(logits)
        losses = jnp.log1p(grown)
        slopes = SCALE * grown / (1.0 + grown)
        if paired:
            slopes = jnp.where(match, -slopes, slopes)
        slopes_ref[rows, :] = slopes.astype(BF16)
        total = losses[:, 0:LANES]
        for c in range(LANES, width, LANES):
            total = total + losses[:, c : c + LANES]
        lanes_ref[rows, :] = total

    @pl.loop(0, first)
    def _(i):
        chunk(i, False)

    @pl.loop(first, first + own // CHUNK)
    def _(i):
        chunk(i, True)

    @pl.loop(first + own // CHUNK, NZ * own // CHUNK)
    def _(i):
        chunk(i, False)

    loss_row = jnp.sum(lanes_ref[...].T, axis=0, keepdims=True)
    low[...] = jnp.dot(slopes_ref[...], txt_all[...], preferred_element_type=F32).astype(BF16)
    row = lax.broadcasted_iota(jnp.int32, (LOSS_ROWS, own), 0)
    tails[...] = jnp.zeros(tails.shape, BF16)
    for z in range(NZ):
        loss = loss_row[:, z * own : (z + 1) * own]
        main = loss.astype(BF16).astype(F32)
        both = jnp.where(row == 0, main, jnp.where(row == 1, loss - main, 0.0))
        tails[z, :, 0:own] = both.astype(BF16)
    tall = own + LOSS_ROWS
    core = place_ref[1]
    for s, bits in enumerate((0, 2 - core, 1 + core, 3)):
        z = place_ref[0] ^ bits
        out_ref = keep if s < 2 else send
        at = s % 2 * tall
        out_ref[at : at + own, :] = low[pl.ds(pl.multiple_of(z * own, CHUNK), own), :]
        out_ref[at + own : at + tall, :] = tails[z]


def slopes_call(place, images, texts):
    rows, features = images.shape
    own = rows // NZ
    cols = len(texts) * own
    return vmem_call(
        slopes_kernel,
        [place, images] + list(texts),
        [shape((rows, cols), BF16)] + [shape((2 * (own + LOSS_ROWS), features), BF16)] * 2,
        18,
        [
            pltpu.VMEM((cols, features), BF16),
            pltpu.VMEM((rows, cols), F32),
            pltpu.VMEM((rows, LANES), F32),
            pltpu.VMEM((rows, features), BF16),
            pltpu.VMEM((NZ, LOSS_ROWS, features), BF16),
        ],
        flops=4 * rows * cols * features,
        transcendentals=3 * rows * cols,
        smem=1,
    )


def text_grads(slopes, images):
    return lax.dot_general(
        slopes, images, (((0,), (0,)), ((), ())), preferred_element_type=F32
    )


def later_parts_kernel(slopes_ref, img_all, stack, *parts):
    own = parts[0].shape[0]
    cols = stack.shape[0]
    start = cols // LANES * LANES
    grads = text_grads(slopes_ref[:, start:], img_all[...]).astype(BF16)
    stack[...] = grads[cols - start :, :]
    for s, part in enumerate(parts):
        at = cols - start + s * own
        part[...] = grads[at : at + own, :]


def now_parts_kernel(slopes_ref, img_all, other, *parts):
    own = parts[0].shape[0]
    cols = other.shape[0]
    grads = text_grads(slopes_ref[:, 0 : -(-cols // LANES) * LANES], img_all[...])
    grads = (grads[0:cols, :] + other[...].astype(F32)).astype(BF16)
    for s, part in enumerate(parts):
        part[...] = grads[s * own : (s + 1) * own, :]


def text_call(body, ins, outs):
    flops = 2 * ins[0].shape[0] * ins[0].shape[1] * ins[1].shape[1] // 2
    return vmem_call(body, ins, outs, 12, flops=flops)


def project(values, grads):
    unit, length = unit_rows(values)
    radial = jnp.sum(unit * grads, axis=-1, keepdims=True)
    return (grads - unit * radial) / length


def far_kernel(mine, theirs, out_ref):
    tall = out_ref.shape[0]
    out_ref[...] = (mine[tall:, :].astype(F32) + theirs[tall:, :].astype(F32)).astype(BF16)


def image_end_kernel(raw_ref, mine, near, far, grad_ref, loss_ref):
    own = raw_ref.shape[0]
    grads = jnp.zeros(raw_ref.shape, F32)
    tail = jnp.zeros((LOSS_ROWS, own), F32)
    for part in (mine, near, far):
        grads = grads + part[0:own, :].astype(F32)
        tail = tail + part[own : own + LOSS_ROWS, 0:own].astype(F32)
    grad_ref[...] = project(raw_ref[...], grads)
    loss_ref[...] = jnp.sum(tail, axis=0, keepdims=True)


def text_end_kernel(raw_ref, base, b, c, d, grad_ref):
    grads = base[...] + b[...].astype(F32)
    grads = grads + c[...].astype(F32) + d[...].astype(F32)
    grad_ref[...] = project(raw_ref[...], grads)


def base_kernel(a, home, out_ref):
    out_ref[...] = a[...].astype(F32) + home[...].astype(F32)


def later_kernel(a, b, c, d, out_ref):
    total = a[...].astype(F32) + b[...].astype(F32)
    total = total + c[...].astype(F32) + d[...].astype(F32)
    out_ref[...] = total.astype(BF16)


def spread_x(value):
    return [value] + [shifted(value, "x", s) for s in HOPS]


def on_device(images, texts):
    own, features = images.shape
    unit = shape((own, features), BF16)
    moved = shifted(texts, BLK, 1)
    spread, txt_low = vmem_call(
        low_kernel, [images, texts], [shape((NZ, own, features), BF16), unit], 8
    )
    img_all = lax.all_to_all(spread, "z", 0, 0).reshape(NZ * own, features)
    now_slots = spread_x(txt_low)
    (moved_low,) = vmem_call(moved_kernel, [moved], [unit], 8, flops=WEIGHT)
    later_slots = spread_x(moved_low)

    place = jnp.stack([lax.axis_index("z"), lax.axis_index("core")]).astype(jnp.int32)
    slopes, keep, send = slopes_call(place, img_all, now_slots + later_slots)
    back_near = across_z(send, 0)
    tall = shape((own + LOSS_ROWS, features), BF16)
    (far_send,) = vmem_call(far_kernel, [keep, back_near], [tall], 8, flops=FAR_WEIGHT)
    back_far = across_z(far_send, 1)
    all_x = shape((NX * own, features), BF16)
    out = text_call(later_parts_kernel, [slopes, img_all], [all_x] + [unit] * NX)
    across = lax.ppermute(out[0], "core", [(1, 0)])
    later_back = [out[1]] + [first_core(p, -s) for p, s in zip(out[2:], HOPS)]
    (later,) = vmem_call(later_kernel, later_back, [unit], 8)
    home = next_group(later, True)
    parts = text_call(now_parts_kernel, [slopes, img_all, across], [unit] * NX)
    now_back = [parts[0]] + [shifted(p, "x", -s) for p, s in zip(parts[1:], HOPS)]

    back_far, home, now_back = lax.optimization_barrier((back_far, home, now_back))
    wide = shape((own, features), F32)
    image_grad, row_loss = vmem_call(
        image_end_kernel, [images, keep, back_near, back_far], [wide, shape((1, own), F32)], 12
    )
    (base,) = vmem_call(base_kernel, [now_back[0], home], [wide], 8, flops=HOME_WEIGHT)
    (text_grad,) = vmem_call(text_end_kernel, [texts, base] + now_back[1:], [wide], 12)
    return (row_loss.reshape(own), image_grad, text_grad)


def solution(mesh):
    groups = mesh.devices.shape[0] // CORES
    fine = Mesh(mesh.devices.reshape(groups, CORES, NX, NZ), BLK + GRP)
    rows = P(BLK + GRP, None)
    return jax.shard_map(
        on_device,
        mesh=fine,
        in_specs=(rows, rows),
        out_specs=(P(BLK + GRP), rows, rows),
        check_vma=False,
    )
```

```python
import jax
import jax.numpy as jnp
from jax import lax
from jax.experimental import pallas as pl
from jax.experimental.pallas import tpu as pltpu
from jax.sharding import Mesh
from jax.sharding import PartitionSpec as P

SCALE = 10.0
SHIFT = -2.0
EPS = 1e-06
CORES, NX, NZ = 2, 4, 4
BLK, GRP = ("g", "core"), ("x", "z")
F32, BF16 = jnp.float32, jnp.bfloat16
MIB = 1024 * 1024
LOSS_ROWS = 16
CHUNK = 16
LANES = 128
HOPS = (2, 1, 3)
WEIGHT = 26_000_000_000
HOME_WEIGHT = 2_000_000_000
END_WEIGHT = 3_000_000_000
FAR_WEIGHT = 10_000_000_000


def shifted(value, axis, steps):
    count = lax.axis_size(axis)
    return lax.ppermute(value, axis, [(i, (i + steps) % count) for i in range(count)])


def across_z(value, step):
    pairs = []
    for core in range(CORES):
        bit = 1 if step == core else 2
        pairs += [(core * NZ + z, core * NZ + (z ^ bit)) for z in range(NZ)]
    return lax.ppermute(value, ("core", "z"), pairs)


def next_group(value, back):
    count = lax.axis_size("g")
    pairs = [(2 * g + 1, 2 * ((g + 1) % count)) for g in range(count)]
    if back:
        pairs = [(b, a) for a, b in pairs]
    return lax.ppermute(value, BLK, pairs)


def turned(value, steps):
    pairs = []
    for core in range(CORES):
        by = steps if core == 0 else -steps
        pairs += [(core * NX + x, core * NX + (x + by) % NX) for x in range(NX)]
    return lax.ppermute(value, ("core", "x"), pairs)


def first_core(value, steps):
    return lax.ppermute(value, ("core", "x"), [(x, (x + steps) % NX) for x in range(NX)])


def vmem_call(body, ins, outs, limit, scratch=(), flops=0, transcendentals=0, smem=0):
    size = sum(a.size * a.dtype.itemsize for a in list(ins) + list(outs))
    return pl.pallas_call(
        body,
        out_shape=list(outs),
        in_specs=[pl.BlockSpec(memory_space=pltpu.SMEM)] * smem
        + [pl.BlockSpec(memory_space=pltpu.VMEM)] * (len(ins) - smem),
        out_specs=[pl.BlockSpec(memory_space=pltpu.VMEM)] * len(outs),
        scratch_shapes=list(scratch),
        compiler_params=pltpu.CompilerParams(vmem_limit_bytes=limit * MIB),
        cost_estimate=pl.CostEstimate(
            flops=flops, bytes_accessed=size, transcendentals=transcendentals
        ),
    )(*ins)


def shape(dims, dtype):
    return jax.ShapeDtypeStruct(dims, dtype)


def unit_rows(values):
    wide = values.astype(F32)
    length = jnp.sqrt(jnp.sum(wide * wide, axis=-1, keepdims=True) + EPS)
    return wide / length, length


def low_kernel(img_ref, txt_ref, spread_ref, low_ref):
    unit, _ = unit_rows(img_ref[...])
    for z in range(NZ):
        spread_ref[z] = unit.astype(BF16)
    unit, _ = unit_rows(txt_ref[...])
    low_ref[...] = unit.astype(BF16)


def moved_kernel(txt_ref, low_ref):
    unit, _ = unit_rows(txt_ref[...])
    low_ref[...] = unit.astype(BF16)


def slopes_kernel(*refs):
    place_ref, img_all, texts = refs[0], refs[1], refs[2:10]
    slopes_ref, keep, send = refs[10:13]
    txt_all, scores, lanes_ref, low, tails = refs[13:18]
    own = img_all.shape[0] // NZ
    first = place_ref[0] * (own // CHUNK)
    for s in range(8):
        txt_all[pl.ds(s * own, own), :] = texts[s][...]
    scores[...] = lax.dot_general(
        img_all[...], txt_all[...], (((1,), (1,)), ((), ())), preferred_element_type=F32
    )
    width = scores.shape[1]

    def chunk(i, paired):
        rows = pl.ds(pl.multiple_of(i * CHUNK, CHUNK), CHUNK)
        logits = scores[rows, :] * SCALE + SHIFT
        if paired:
            row = lax.broadcasted_iota(jnp.int32, logits.shape, 0) + (i - first) * CHUNK
            col = lax.broadcasted_iota(jnp.int32, logits.shape, 1)
            match = row == col
            logits = jnp.where(match, -logits, logits)
        grown = jnp.exp(logits)
        losses = jnp.log1p(grown)
        slopes = SCALE * grown / (1.0 + grown)
        if paired:
            slopes = jnp.where(match, -slopes, slopes)
        slopes_ref[rows, :] = slopes.astype(BF16)
        total = losses[:, 0:LANES]
        for c in range(LANES, width, LANES):
            total = total + losses[:, c : c + LANES]
        lanes_ref[rows, :] = total

    @pl.loop(0, first)
    def _(i):
        chunk(i, False)

    @pl.loop(first, first + own // CHUNK)
    def _(i):
        chunk(i, True)

    @pl.loop(first + own // CHUNK, NZ * own // CHUNK)
    def _(i):
        chunk(i, False)

    loss_row = jnp.sum(lanes_ref[...].T, axis=0, keepdims=True)
    low[...] = jnp.dot(slopes_ref[...], txt_all[...], preferred_element_type=F32).astype(BF16)
    row = lax.broadcasted_iota(jnp.int32, (LOSS_ROWS, own), 0)
    tails[...] = jnp.zeros(tails.shape, BF16)
    for z in range(NZ):
        loss = loss_row[:, z * own : (z + 1) * own]
        main = loss.astype(BF16).astype(F32)
        both = jnp.where(row == 0, main, jnp.where(row == 1, loss - main, 0.0))
        tails[z, :, 0:own] = both.astype(BF16)
    tall = own + LOSS_ROWS
    core = place_ref[1]
    for s, bits in enumerate((0, 2 - core, 1 + core, 3)):
        z = place_ref[0] ^ bits
        out_ref = keep if s < 2 else send
        at = s % 2 * tall
        out_ref[at : at + own, :] = low[pl.ds(pl.multiple_of(z * own, CHUNK), own), :]
        out_ref[at + own : at + tall, :] = tails[z]


def slopes_call(place, images, texts):
    rows, features = images.shape
    own = rows // NZ
    cols = len(texts) * own
    return vmem_call(
        slopes_kernel,
        [place, images] + list(texts),
        [shape((rows, cols), BF16)] + [shape((2 * (own + LOSS_ROWS), features), BF16)] * 2,
        18,
        [
            pltpu.VMEM((cols, features), BF16),
            pltpu.VMEM((rows, cols), F32),
            pltpu.VMEM((rows, LANES), F32),
            pltpu.VMEM((rows, features), BF16),
            pltpu.VMEM((NZ, LOSS_ROWS, features), BF16),
        ],
        flops=4 * rows * cols * features,
        transcendentals=3 * rows * cols,
        smem=1,
    )


def text_grads(slopes, images):
    return lax.dot_general(
        slopes, images, (((0,), (0,)), ((), ())), preferred_element_type=F32
    )


def later_parts_kernel(slopes_ref, img_all, stack, *parts):
    own = parts[0].shape[0]
    cols = stack.shape[0]
    start = cols // LANES * LANES
    grads = text_grads(slopes_ref[:, start:], img_all[...]).astype(BF16)
    stack[...] = grads[cols - start :, :]
    for s, part in enumerate(parts):
        at = cols - start + s * own
        part[...] = grads[at : at + own, :]


def now_parts_kernel(slopes_ref, img_all, other, *parts):
    own = parts[0].shape[0]
    cols = other.shape[0]
    grads = text_grads(slopes_ref[:, 0 : -(-cols // LANES) * LANES], img_all[...])
    grads = (grads[0:cols, :] + other[...].astype(F32)).astype(BF16)
    for s, part in enumerate(parts):
        part[...] = grads[s * own : (s + 1) * own, :]


def text_call(body, ins, outs):
    flops = 2 * ins[0].shape[0] * ins[0].shape[1] * ins[1].shape[1] // 2
    return vmem_call(body, ins, outs, 12, flops=flops)


def project(values, grads):
    unit, length = unit_rows(values)
    radial = jnp.sum(unit * grads, axis=-1, keepdims=True)
    return (grads - unit * radial) / length


def far_kernel(mine, theirs, out_ref):
    tall = out_ref.shape[0]
    out_ref[...] = (mine[tall:, :].astype(F32) + theirs[tall:, :].astype(F32)).astype(BF16)


def image_end_kernel(raw_ref, mine, near, far, grad_ref, loss_ref):
    own = raw_ref.shape[0]
    grads = jnp.zeros(raw_ref.shape, F32)
    tail = jnp.zeros((LOSS_ROWS, own), F32)
    for part in (mine, near, far):
        grads = grads + part[0:own, :].astype(F32)
        tail = tail + part[own : own + LOSS_ROWS, 0:own].astype(F32)
    grad_ref[...] = project(raw_ref[...], grads)
    loss_ref[...] = jnp.sum(tail, axis=0, keepdims=True)


def text_end_kernel(raw_ref, base, b, c, d, grad_ref):
    grads = base[...] + b[...].astype(F32)
    grads = grads + c[...].astype(F32) + d[...].astype(F32)
    grad_ref[...] = project(raw_ref[...], grads)


def base_kernel(a, home, out_ref):
    out_ref[...] = a[...].astype(F32) + home[...].astype(F32)


def later_kernel(a, b, c, d, out_ref):
    total = a[...].astype(F32) + b[...].astype(F32)
    total = total + c[...].astype(F32) + d[...].astype(F32)
    out_ref[...] = total.astype(BF16)


def spread_x(value):
    return [value] + [shifted(value, "x", s) for s in HOPS]


def on_device(images, texts):
    own, features = images.shape
    unit = shape((own, features), BF16)
    moved = shifted(texts, BLK, 1)
    spread, txt_low = vmem_call(
        low_kernel, [images, texts], [shape((NZ, own, features), BF16), unit], 8
    )
    img_all = lax.all_to_all(spread, "z", 0, 0).reshape(NZ * own, features)
    after, before = turned(txt_low, 1), turned(txt_low, -1)
    beyond = turned(after, 1)
    now_slots = [txt_low, beyond, after, before]
    (moved_low,) = vmem_call(moved_kernel, [moved], [unit], 8, flops=WEIGHT)
    later_slots = spread_x(moved_low)

    place = jnp.stack([lax.axis_index("z"), lax.axis_index("core")]).astype(jnp.int32)
    slopes, keep, send = slopes_call(place, img_all, now_slots + later_slots)
    back_near = across_z(send, 0)
    tall = shape((own + LOSS_ROWS, features), BF16)
    (far_send,) = vmem_call(far_kernel, [keep, back_near], [tall], 8, flops=FAR_WEIGHT)
    back_far = across_z(far_send, 1)
    all_x = shape((NX * own, features), BF16)
    out = text_call(later_parts_kernel, [slopes, img_all], [all_x] + [unit] * NX)
    across = lax.ppermute(out[0], "core", [(1, 0)])
    later_back = [out[1]] + [first_core(p, -s) for p, s in zip(out[2:], HOPS)]
    (later,) = vmem_call(later_kernel, later_back, [unit], 8)
    home = next_group(later, True)
    parts = text_call(now_parts_kernel, [slopes, img_all, across], [unit] * NX)
    now_back = [parts[0]] + [turned(p, -s) for p, s in zip(parts[1:], HOPS)]

    wide = shape((own, features), F32)
    image_grad, row_loss = vmem_call(
        image_end_kernel, [images, keep, back_near, back_far], [wide, shape((1, own), F32)], 12, flops=END_WEIGHT
    )
    home, image_grad = lax.optimization_barrier((home, image_grad))
    (base,) = vmem_call(base_kernel, [now_back[0], home], [wide], 8, flops=HOME_WEIGHT)
    (text_grad,) = vmem_call(text_end_kernel, [texts, base] + now_back[1:], [wide], 12)
    return (row_loss.reshape(own), image_grad, text_grad)


def solution(mesh):
    groups = mesh.devices.shape[0] // CORES
    fine = Mesh(mesh.devices.reshape(groups, CORES, NX, NZ), BLK + GRP)
    rows = P(BLK + GRP, None)
    return jax.shard_map(
        on_device,
        mesh=fine,
        in_specs=(rows, rows),
        out_specs=(P(BLK + GRP), rows, rows),
        check_vma=False,
    )
```

```python
import jax
import jax.numpy as jnp
from jax import lax
from jax.experimental import pallas as pl
from jax.experimental.pallas import tpu as pltpu
from jax.sharding import Mesh
from jax.sharding import PartitionSpec as P

SCALE = 10.0
SHIFT = -2.0
EPS = 1e-06
CORES, NX, NZ = 2, 4, 4
BLK, GRP = ("g", "core"), ("x", "z")
F32, BF16 = jnp.float32, jnp.bfloat16
MIB = 1024 * 1024
LOSS_ROWS = 16
CHUNK = 16
LANES = 128
GROUP = 384
HOPS = (2, 1, 3)
WEIGHT = 26_000_000_000
HOME_WEIGHT = 4_000_000_000
FAR_WEIGHT = 10_000_000_000


def shifted(value, axis, steps):
    count = lax.axis_size(axis)
    return lax.ppermute(value, axis, [(i, (i + steps) % count) for i in range(count)])


def across_z(value, step):
    pairs = []
    for core in range(CORES):
        bit = 1 if step == core else 2
        pairs += [(core * NZ + z, core * NZ + (z ^ bit)) for z in range(NZ)]
    return lax.ppermute(value, ("core", "z"), pairs)


def next_group(value, back):
    count = lax.axis_size("g")
    pairs = [(2 * g + 1, 2 * ((g + 1) % count)) for g in range(count)]
    if back:
        pairs = [(b, a) for a, b in pairs]
    return lax.ppermute(value, BLK, pairs)


def first_core(value, steps):
    return lax.ppermute(value, ("core", "x"), [(x, (x + steps) % NX) for x in range(NX)])


def vmem_call(body, ins, outs, limit, scratch=(), flops=0, transcendentals=0, smem=0):
    size = sum(a.size * a.dtype.itemsize for a in list(ins) + list(outs))
    return pl.pallas_call(
        body,
        out_shape=list(outs),
        in_specs=[pl.BlockSpec(memory_space=pltpu.SMEM)] * smem
        + [pl.BlockSpec(memory_space=pltpu.VMEM)] * (len(ins) - smem),
        out_specs=[pl.BlockSpec(memory_space=pltpu.VMEM)] * len(outs),
        scratch_shapes=list(scratch),
        compiler_params=pltpu.CompilerParams(vmem_limit_bytes=limit * MIB),
        cost_estimate=pl.CostEstimate(
            flops=flops, bytes_accessed=size, transcendentals=transcendentals
        ),
    )(*ins)


def shape(dims, dtype):
    return jax.ShapeDtypeStruct(dims, dtype)


def unit_rows(values):
    wide = values.astype(F32)
    length = jnp.sqrt(jnp.sum(wide * wide, axis=-1, keepdims=True) + EPS)
    return wide / length, length


def low_kernel(img_ref, txt_ref, spread_ref, low_ref):
    unit, _ = unit_rows(img_ref[...])
    for z in range(NZ):
        spread_ref[z] = unit.astype(BF16)
    unit, _ = unit_rows(txt_ref[...])
    low_ref[...] = unit.astype(BF16)


def moved_kernel(txt_ref, low_ref):
    unit, _ = unit_rows(txt_ref[...])
    low_ref[...] = unit.astype(BF16)


def slopes_kernel(*refs):
    place_ref, img_all, texts = refs[0], refs[1], refs[2:10]
    slopes_ref, keep, send = refs[10:13]
    txt_all, scores, lanes_ref, low, tails = refs[13:18]
    own = img_all.shape[0] // NZ
    first = place_ref[0] * (own // CHUNK)
    for s in range(8):
        txt_all[pl.ds(s * own, own), :] = texts[s][...]
    scores[...] = lax.dot_general(
        img_all[...], txt_all[...], (((1,), (1,)), ((), ())), preferred_element_type=F32
    )
    width = scores.shape[1]

    def chunk(i, paired):
        rows = pl.ds(pl.multiple_of(i * CHUNK, CHUNK), CHUNK)
        total = jnp.zeros((CHUNK, LANES), F32)
        for c in range(0, width, GROUP):
            logits = scores[rows, c : c + GROUP] * SCALE + SHIFT
            masked = paired and c == 0
            if masked:
                row = lax.broadcasted_iota(jnp.int32, logits.shape, 0) + (i - first) * CHUNK
                col = lax.broadcasted_iota(jnp.int32, logits.shape, 1)
                match = row == col
                logits = jnp.where(match, -logits, logits)
            grown = jnp.exp(logits)
            losses = jnp.log1p(grown)
            slopes = SCALE * grown / (1.0 + grown)
            if masked:
                slopes = jnp.where(match, -slopes, slopes)
            slopes_ref[rows, c : c + GROUP] = slopes.astype(BF16)
            for at in range(0, GROUP, LANES):
                total = total + losses[:, at : at + LANES]
        lanes_ref[rows, :] = total

    @pl.loop(0, first)
    def _(i):
        chunk(i, False)

    @pl.loop(first, first + own // CHUNK)
    def _(i):
        chunk(i, True)

    @pl.loop(first + own // CHUNK, NZ * own // CHUNK)
    def _(i):
        chunk(i, False)

    loss_row = jnp.sum(lanes_ref[...].T, axis=0, keepdims=True)
    low[...] = jnp.dot(slopes_ref[...], txt_all[...], preferred_element_type=F32).astype(BF16)
    row = lax.broadcasted_iota(jnp.int32, (LOSS_ROWS, own), 0)
    tails[...] = jnp.zeros(tails.shape, BF16)
    for z in range(NZ):
        loss = loss_row[:, z * own : (z + 1) * own]
        main = loss.astype(BF16).astype(F32)
        both = jnp.where(row == 0, main, jnp.where(row == 1, loss - main, 0.0))
        tails[z, :, 0:own] = both.astype(BF16)
    tall = own + LOSS_ROWS
    core = place_ref[1]
    for s, bits in enumerate((0, 2 - core, 1 + core, 3)):
        z = place_ref[0] ^ bits
        out_ref = keep if s < 2 else send
        at = s % 2 * tall
        out_ref[at : at + own, :] = low[pl.ds(pl.multiple_of(z * own, CHUNK), own), :]
        out_ref[at + own : at + tall, :] = tails[z]


def slopes_call(place, images, texts):
    rows, features = images.shape
    own = rows // NZ
    cols = len(texts) * own
    return vmem_call(
        slopes_kernel,
        [place, images] + list(texts),
        [shape((rows, cols), BF16)] + [shape((2 * (own + LOSS_ROWS), features), BF16)] * 2,
        18,
        [
            pltpu.VMEM((cols, features), BF16),
            pltpu.VMEM((rows, cols), F32),
            pltpu.VMEM((rows, LANES), F32),
            pltpu.VMEM((rows, features), BF16),
            pltpu.VMEM((NZ, LOSS_ROWS, features), BF16),
        ],
        flops=4 * rows * cols * features,
        transcendentals=3 * rows * cols,
        smem=1,
    )


def text_grads(slopes, images):
    return lax.dot_general(
        slopes, images, (((0,), (0,)), ((), ())), preferred_element_type=F32
    )


def later_parts_kernel(slopes_ref, img_all, stack, *parts):
    own = parts[0].shape[0]
    cols = stack.shape[0]
    start = cols // LANES * LANES
    grads = text_grads(slopes_ref[:, start:], img_all[...]).astype(BF16)
    stack[...] = grads[cols - start :, :]
    for s, part in enumerate(parts):
        at = cols - start + s * own
        part[...] = grads[at : at + own, :]


def now_parts_kernel(slopes_ref, img_all, other, *parts):
    own = parts[0].shape[0]
    cols = other.shape[0]
    grads = text_grads(slopes_ref[:, 0 : -(-cols // LANES) * LANES], img_all[...])
    grads = (grads[0:cols, :] + other[...].astype(F32)).astype(BF16)
    for s, part in enumerate(parts):
        part[...] = grads[s * own : (s + 1) * own, :]


def text_call(body, ins, outs):
    flops = 2 * ins[0].shape[0] * ins[0].shape[1] * ins[1].shape[1] // 2
    return vmem_call(body, ins, outs, 12, flops=flops)


def project(values, grads):
    unit, length = unit_rows(values)
    radial = jnp.sum(unit * grads, axis=-1, keepdims=True)
    return (grads - unit * radial) / length


def far_kernel(mine, theirs, out_ref):
    tall = out_ref.shape[0]
    out_ref[...] = (mine[tall:, :].astype(F32) + theirs[tall:, :].astype(F32)).astype(BF16)


def image_end_kernel(raw_ref, mine, near, far, grad_ref, loss_ref):
    own = raw_ref.shape[0]
    grads = jnp.zeros(raw_ref.shape, F32)
    tail = jnp.zeros((LOSS_ROWS, own), F32)
    for part in (mine, near, far):
        grads = grads + part[0:own, :].astype(F32)
        tail = tail + part[own : own + LOSS_ROWS, 0:own].astype(F32)
    grad_ref[...] = project(raw_ref[...], grads)
    loss_ref[...] = jnp.sum(tail, axis=0, keepdims=True)


def text_end_kernel(raw_ref, base, b, c, d, grad_ref):
    grads = base[...] + b[...].astype(F32)
    grads = grads + c[...].astype(F32) + d[...].astype(F32)
    grad_ref[...] = project(raw_ref[...], grads)


def base_kernel(a, home, out_ref):
    out_ref[...] = a[...].astype(F32) + home[...].astype(F32)


def later_kernel(a, b, c, d, out_ref):
    total = a[...].astype(F32) + b[...].astype(F32)
    total = total + c[...].astype(F32) + d[...].astype(F32)
    out_ref[...] = total.astype(BF16)


def spread_x(value):
    return [value] + [shifted(value, "x", s) for s in HOPS]


def on_device(images, texts):
    own, features = images.shape
    unit = shape((own, features), BF16)
    moved = shifted(texts, BLK, 1)
    spread, txt_low = vmem_call(
        low_kernel, [images, texts], [shape((NZ, own, features), BF16), unit], 8
    )
    img_all = lax.all_to_all(spread, "z", 0, 0).reshape(NZ * own, features)
    now_slots = spread_x(txt_low)
    (moved_low,) = vmem_call(moved_kernel, [moved], [unit], 8, flops=WEIGHT)
    later_slots = spread_x(moved_low)

    place = jnp.stack([lax.axis_index("z"), lax.axis_index("core")]).astype(jnp.int32)
    slopes, keep, send = slopes_call(place, img_all, now_slots + later_slots)
    back_near = across_z(send, 0)
    tall = shape((own + LOSS_ROWS, features), BF16)
    (far_send,) = vmem_call(far_kernel, [keep, back_near], [tall], 8, flops=FAR_WEIGHT)
    back_far = across_z(far_send, 1)
    all_x = shape((NX * own, features), BF16)
    out = text_call(later_parts_kernel, [slopes, img_all], [all_x] + [unit] * NX)
    across = lax.ppermute(out[0], "core", [(1, 0)])
    later_back = [out[1]] + [first_core(p, -s) for p, s in zip(out[2:], HOPS)]
    (later,) = vmem_call(later_kernel, later_back, [unit], 8)
    home = next_group(later, True)
    parts = text_call(now_parts_kernel, [slopes, img_all, across], [unit] * NX)
    now_back = [parts[0]] + [shifted(p, "x", -s) for p, s in zip(parts[1:], HOPS)]

    back_far, home, now_back = lax.optimization_barrier((back_far, home, now_back))
    wide = shape((own, features), F32)
    image_grad, row_loss = vmem_call(
        image_end_kernel, [images, keep, back_near, back_far], [wide, shape((1, own), F32)], 12
    )
    (base,) = vmem_call(base_kernel, [now_back[0], home], [wide], 8, flops=HOME_WEIGHT)
    (text_grad,) = vmem_call(text_end_kernel, [texts, base] + now_back[1:], [wide], 12)
    return (row_loss.reshape(own), image_grad, text_grad)


def solution(mesh):
    groups = mesh.devices.shape[0] // CORES
    fine = Mesh(mesh.devices.reshape(groups, CORES, NX, NZ), BLK + GRP)
    rows = P(BLK + GRP, None)
    return jax.shard_map(
        on_device,
        mesh=fine,
        in_specs=(rows, rows),
        out_specs=(P(BLK + GRP), rows, rows),
        check_vma=False,
    )
```

```python
import jax
import jax.numpy as jnp
from jax import lax
from jax.experimental import pallas as pl
from jax.experimental.pallas import tpu as pltpu
from jax.sharding import Mesh
from jax.sharding import PartitionSpec as P

SCALE = 10.0
SHIFT = -2.0
EPS = 1e-06
CORES, NX, NZ = 2, 4, 4
BLK, GRP = ("g", "core"), ("x", "z")
F32, BF16 = jnp.float32, jnp.bfloat16
MIB = 1024 * 1024
LOSS_ROWS = 16
CHUNK = 16
LANES = 128
GROUP = 384
HOPS = (2, 1, 3)
WEIGHT = 26_000_000_000
HOME_WEIGHT = 4_000_000_000
FAR_WEIGHT = 10_000_000_000


def shifted(value, axis, steps):
    count = lax.axis_size(axis)
    return lax.ppermute(value, axis, [(i, (i + steps) % count) for i in range(count)])


def across_z(value, step):
    pairs = []
    for core in range(CORES):
        bit = 1 if step == core else 2
        pairs += [(core * NZ + z, core * NZ + (z ^ bit)) for z in range(NZ)]
    return lax.ppermute(value, ("core", "z"), pairs)


def next_group(value, back):
    count = lax.axis_size("g")
    pairs = [(2 * g + 1, 2 * ((g + 1) % count)) for g in range(count)]
    if back:
        pairs = [(b, a) for a, b in pairs]
    return lax.ppermute(value, BLK, pairs)


def first_core(value, steps):
    return lax.ppermute(value, ("core", "x"), [(x, (x + steps) % NX) for x in range(NX)])


def vmem_call(body, ins, outs, limit, scratch=(), flops=0, transcendentals=0, smem=0):
    size = sum(a.size * a.dtype.itemsize for a in list(ins) + list(outs))
    return pl.pallas_call(
        body,
        out_shape=list(outs),
        in_specs=[pl.BlockSpec(memory_space=pltpu.SMEM)] * smem
        + [pl.BlockSpec(memory_space=pltpu.VMEM)] * (len(ins) - smem),
        out_specs=[pl.BlockSpec(memory_space=pltpu.VMEM)] * len(outs),
        scratch_shapes=list(scratch),
        compiler_params=pltpu.CompilerParams(vmem_limit_bytes=limit * MIB),
        cost_estimate=pl.CostEstimate(
            flops=flops, bytes_accessed=size, transcendentals=transcendentals
        ),
    )(*ins)


def shape(dims, dtype):
    return jax.ShapeDtypeStruct(dims, dtype)


def unit_rows(values):
    wide = values.astype(F32)
    length = jnp.sqrt(jnp.sum(wide * wide, axis=-1, keepdims=True) + EPS)
    return wide / length, length


def low_kernel(img_ref, txt_ref, spread_ref, low_ref):
    unit, _ = unit_rows(img_ref[...])
    for z in range(NZ):
        spread_ref[z] = unit.astype(BF16)
    unit, _ = unit_rows(txt_ref[...])
    low_ref[...] = unit.astype(BF16)


def moved_kernel(txt_ref, low_ref):
    unit, _ = unit_rows(txt_ref[...])
    low_ref[...] = unit.astype(BF16)


def slopes_kernel(*refs):
    place_ref, img_all, texts = refs[0], refs[1], refs[2:10]
    slopes_ref, keep, send = refs[10:13]
    txt_all, scores, lanes_ref, low, tails = refs[13:18]
    own = img_all.shape[0] // NZ
    first = place_ref[0] * (own // CHUNK)
    for s in range(8):
        txt_all[pl.ds(s * own, own), :] = texts[s][...]
    scores[...] = lax.dot_general(
        img_all[...], txt_all[...], (((1,), (1,)), ((), ())), preferred_element_type=F32
    )
    width = scores.shape[1]

    def chunk(i, paired):
        rows = pl.ds(pl.multiple_of(i * CHUNK, CHUNK), CHUNK)
        total = jnp.zeros((CHUNK, LANES), F32)
        for c in range(0, width, GROUP):
            logits = scores[rows, c : c + GROUP] * SCALE + SHIFT
            masked = paired and c == 0
            if masked:
                row = lax.broadcasted_iota(jnp.int32, logits.shape, 0) + (i - first) * CHUNK
                col = lax.broadcasted_iota(jnp.int32, logits.shape, 1)
                match = row == col
                logits = jnp.where(match, -logits, logits)
            grown = jnp.exp(logits)
            losses = jnp.log1p(grown)
            slopes = SCALE * grown / (1.0 + grown)
            if masked:
                slopes = jnp.where(match, -slopes, slopes)
            slopes_ref[rows, c : c + GROUP] = slopes.astype(BF16)
            for at in range(0, GROUP, LANES):
                total = total + losses[:, at : at + LANES]
        lanes_ref[rows, :] = total

    @pl.loop(0, first)
    def _(i):
        chunk(i, False)

    @pl.loop(first, first + own // CHUNK)
    def _(i):
        chunk(i, True)

    @pl.loop(first + own // CHUNK, NZ * own // CHUNK)
    def _(i):
        chunk(i, False)

    loss_row = jnp.sum(lanes_ref[...].T, axis=0, keepdims=True)
    low[...] = jnp.dot(slopes_ref[...], txt_all[...], preferred_element_type=F32).astype(BF16)
    row = lax.broadcasted_iota(jnp.int32, (LOSS_ROWS, own), 0)
    tails[...] = jnp.zeros(tails.shape, BF16)
    for z in range(NZ):
        loss = loss_row[:, z * own : (z + 1) * own]
        main = loss.astype(BF16).astype(F32)
        both = jnp.where(row == 0, main, jnp.where(row == 1, loss - main, 0.0))
        tails[z, :, 0:own] = both.astype(BF16)
    tall = own + LOSS_ROWS
    core = place_ref[1]
    for s, bits in enumerate((0, 2 - core, 1 + core, 3)):
        z = place_ref[0] ^ bits
        out_ref = keep if s < 2 else send
        at = s % 2 * tall
        out_ref[at : at + own, :] = low[pl.ds(pl.multiple_of(z * own, CHUNK), own), :]
        out_ref[at + own : at + tall, :] = tails[z]


def slopes_call(place, images, texts):
    rows, features = images.shape
    own = rows // NZ
    cols = len(texts) * own
    return vmem_call(
        slopes_kernel,
        [place, images] + list(texts),
        [shape((rows, cols), BF16)] + [shape((2 * (own + LOSS_ROWS), features), BF16)] * 2,
        18,
        [
            pltpu.VMEM((cols, features), BF16),
            pltpu.VMEM((rows, cols), F32),
            pltpu.VMEM((rows, LANES), F32),
            pltpu.VMEM((rows, features), BF16),
            pltpu.VMEM((NZ, LOSS_ROWS, features), BF16),
        ],
        flops=4 * rows * cols * features,
        transcendentals=3 * rows * cols,
        smem=1,
    )


def text_grads(slopes, images):
    return lax.dot_general(
        slopes, images, (((0,), (0,)), ((), ())), preferred_element_type=F32
    )


def later_parts_kernel(slopes_ref, img_all, stack, *parts):
    own = parts[0].shape[0]
    cols = stack.shape[0]
    start = cols // LANES * LANES
    grads = text_grads(slopes_ref[:, start:], img_all[...]).astype(BF16)
    stack[...] = grads[cols - start :, :]
    for s, part in enumerate(parts):
        at = cols - start + s * own
        part[...] = grads[at : at + own, :]


def now_parts_kernel(slopes_ref, img_all, other, *parts):
    own = parts[0].shape[0]
    cols = other.shape[0]
    grads = text_grads(slopes_ref[:, 0 : -(-cols // LANES) * LANES], img_all[...])
    grads = (grads[0:cols, :] + other[...].astype(F32)).astype(BF16)
    for s, part in enumerate(parts):
        part[...] = grads[s * own : (s + 1) * own, :]


def text_call(body, ins, outs):
    flops = 2 * ins[0].shape[0] * ins[0].shape[1] * ins[1].shape[1] // 2
    return vmem_call(body, ins, outs, 12, flops=flops)


def project(values, grads):
    unit, length = unit_rows(values)
    radial = jnp.sum(unit * grads, axis=-1, keepdims=True)
    return (grads - unit * radial) / length


def far_kernel(mine, theirs, out_ref):
    tall = out_ref.shape[0]
    out_ref[...] = (mine[tall:, :].astype(F32) + theirs[tall:, :].astype(F32)).astype(BF16)


def image_end_kernel(raw_ref, mine, near, far, grad_ref, loss_ref):
    own = raw_ref.shape[0]
    grads = jnp.zeros(raw_ref.shape, F32)
    tail = jnp.zeros((LOSS_ROWS, own), F32)
    for part in (mine, near, far):
        grads = grads + part[0:own, :].astype(F32)
        tail = tail + part[own : own + LOSS_ROWS, 0:own].astype(F32)
    grad_ref[...] = project(raw_ref[...], grads)
    loss_ref[...] = jnp.sum(tail, axis=0, keepdims=True)


def text_end_kernel(raw_ref, base, b, c, d, grad_ref):
    grads = base[...] + b[...].astype(F32)
    grads = grads + c[...].astype(F32) + d[...].astype(F32)
    grad_ref[...] = project(raw_ref[...], grads)


def base_kernel(a, home, out_ref):
    out_ref[...] = a[...].astype(F32) + home[...].astype(F32)


def later_kernel(a, b, c, d, out_ref):
    total = a[...].astype(F32) + b[...].astype(F32)
    total = total + c[...].astype(F32) + d[...].astype(F32)
    out_ref[...] = total.astype(BF16)


def spread_x(value):
    return [value] + [shifted(value, "x", s) for s in HOPS]


def on_device(images, texts):
    own, features = images.shape
    unit = shape((own, features), BF16)
    moved = shifted(texts, BLK, 1)
    spread, txt_low = vmem_call(
        low_kernel, [images, texts], [shape((NZ, own, features), BF16), unit], 8
    )
    img_all = lax.all_to_all(spread, "z", 0, 0).reshape(NZ * own, features)
    now_slots = spread_x(txt_low)
    (moved_low,) = vmem_call(moved_kernel, [moved], [unit], 8, flops=WEIGHT)
    later_slots = spread_x(moved_low)

    place = jnp.stack([lax.axis_index("z"), lax.axis_index("core")]).astype(jnp.int32)
    slopes, keep, send = slopes_call(place, img_all, now_slots + later_slots)
    back_near = across_z(send, 0)
    tall = shape((own + LOSS_ROWS, features), BF16)
    (far_send,) = vmem_call(far_kernel, [keep, back_near], [tall], 8, flops=FAR_WEIGHT)
    back_far = across_z(far_send, 1)
    all_x = shape((NX * own, features), BF16)
    out = text_call(later_parts_kernel, [slopes, img_all], [all_x] + [unit] * NX)
    across = lax.ppermute(out[0], "core", [(1, 0)])
    later_back = [out[1]] + [first_core(p, -s) for p, s in zip(out[2:], HOPS)]
    (later,) = vmem_call(later_kernel, later_back, [unit], 8)
    home = next_group(later, True)
    parts = text_call(now_parts_kernel, [slopes, img_all, across], [unit] * NX)
    now_back = [parts[0]] + [shifted(p, "x", -s) for p, s in zip(parts[1:], HOPS)]

    wide = shape((own, features), F32)
    (base,) = vmem_call(base_kernel, [now_back[0], home], [wide], 8, flops=HOME_WEIGHT)
    (text_grad,) = vmem_call(text_end_kernel, [texts, base] + now_back[1:], [wide], 12)
    back_far, text_grad = lax.optimization_barrier((back_far, text_grad))
    image_grad, row_loss = vmem_call(
        image_end_kernel, [images, keep, back_near, back_far], [wide, shape((1, own), F32)], 12
    )
    return (row_loss.reshape(own), image_grad, text_grad)


def solution(mesh):
    groups = mesh.devices.shape[0] // CORES
    fine = Mesh(mesh.devices.reshape(groups, CORES, NX, NZ), BLK + GRP)
    rows = P(BLK + GRP, None)
    return jax.shard_map(
        on_device,
        mesh=fine,
        in_specs=(rows, rows),
        out_specs=(P(BLK + GRP), rows, rows),
        check_vma=False,
    )
```
